32 devices in a mesh: neg: 8 (over z, y), rep: 4 (over x, core).
Axes of the slice: x: 2, y: 2, z: 4, core: 2. Of those that a mesh axis runs over, the one named last changes fastest.
Arguments:
- goal_states: bfloat16 [4, 64, 128, 512], P('rep', 'neg'), may hold values from -6 to 6
- premise_states: bfloat16 [4, 256, 128, 512], P('rep', 'neg'), may hold values from -6 to 6
- goal_ids: int32 [4, 64, 128], P('rep', 'neg'), may hold values from 0 to 31999, as said below
- premise_ids: int32 [4, 256, 128], P('rep', 'neg'), may hold values from 0 to 31999, as said below
- positives: int32 [4, 64], P('rep'), may hold values from 0 to 255
- depthwise_kernels: float32 [2, 3, 512], replicated, may hold values from -3.5 to 3.5
- block_norm_gains: float32 [2, 512], replicated, may hold values from 0.25 to 1.75
- pointwise_weights: bfloat16 [2, 512, 512], replicated, may hold values from -0.25 to 0.25
- head_weight: bfloat16 [512, 256], replicated, may hold values from -0.25 to 0.25
Outputs:
- goal_loss: float32 [4, 64], P('rep', 'neg')
- grad_depth: float32 [2, 3, 512], replicated
- grad_gain: float32 [2, 512], replicated
- grad_point: float32 [2, 512, 512], replicated
- grad_head: float32 [512, 256], replicated
The draws below stay inside these ranges and needn't reach their ends.
Inputs may be any that keep to these rules, and one draw needn't show every extreme that they name: `goal_ids`: id 0 marks padding: a sequence's ids are nonzero on its first positions and 0 after them, with at least 16 nonzero ids. `premise_ids`: id 0 marks padding: a sequence's ids are nonzero on its first positions and 0 after them, with at least 16 nonzero ids.
All inputs are finite; a program needn't handle non-finite values.
Results may differ from the reference program's by a relative error of at most 0.022.
Values may be sent and summed in bfloat16 or wider, within the bound.
A program may use at most 192 MiB of HBM per device.

```python
import jax
import jax.numpy as jnp
from jax import lax

D = 512
E = 256
L = 128
K = 3
LOWER_DILATION = 4
UPPER_DILATION = 8
VOCAB = 32000
G_DEV = 8
P_DEV = 32
GOALS_GRP = 64
PREM_GRP = 256
N_NEG = 8
N_REP = 4


def padded_ids(key, leading):
    key_length, key_token = jax.random.split(key)
    lengths = jax.random.randint(key_length, leading, L // 8, L + 1)
    tokens = jax.random.randint(key_token, leading + (L,), 1, VOCAB)
    places = jnp.arange(L)
    return jnp.where(places < lengths[..., None], tokens, 0).astype(jnp.int32)


def draw_goal_ids(key, part):
    return padded_ids(jax.random.fold_in(key, 11), (N_REP, GOALS_GRP))


def draw_premise_ids(key, part):
    return padded_ids(jax.random.fold_in(key, 23), (N_REP, PREM_GRP))


def set_ends(result, key, smallest, high):
    longest = result.shape.index(max(result.shape))
    spots = []
    for shift in (0, 1):
        where = [jax.random.randint(jax.random.fold_in(key, axis), (), 0, length) for axis, length in enumerate(result.shape)]
        where[longest] = (where[longest] + shift) % result.shape[longest]
        spots.append(tuple(where))
    return result.at[spots[0]].set(smallest).at[spots[1]].set(high)


def with_spikes(entries, stream_key, source, target, shards_of, factor):
    def block_of(position):
        return (jnp.arange(entries.shape[position]) // (entries.shape[position] // shards_of)).reshape((-1,) + (1,) * (entries.ndim - 1 - position))

    near = jax.random.permutation(stream_key, shards_of)[block_of(target)]
    other_side = (block_of(target) + shards_of // 2) % shards_of
    return jnp.where((block_of(source) == near) | (block_of(source) == other_side), factor * entries, entries)


def steps_of(key, dims, pieces, low, largest):
    factor_of, own = 1.0, jax.random.fold_in(key, 6)
    for dim, shards_of in pieces:
        draws = jnp.exp(jax.random.uniform(jax.random.fold_in(own, dim), (shards_of,), jnp.float32, low / len(pieces), largest / len(pieces)))
        factor_of = factor_of * jnp.repeat(draws, dims[dim] // shards_of).reshape([-1 if axis == dim else 1 for axis in range(len(dims))])
    return factor_of


def gaussian(key, extent, spread, limit, cuts=(), kind=jnp.bfloat16):
    drawn = jax.random.normal(key, extent, jnp.float32) * spread
    if len(cuts) > 0:
        drawn = steps_of(key, extent, cuts, -0.22, 0.18) * drawn
    return jnp.clip(drawn, min=-limit, max=limit).astype(kind)


def noise_with(rng, extent, deviation, bound, pieces, heavy, kind=jnp.bfloat16):
    drawn = deviation * jax.random.normal(rng, extent, jnp.float32)
    if pieces:
        drawn = drawn * steps_of(rng, extent, pieces, -0.22, 0.18)
    return jnp.clip(with_spikes(drawn, jax.random.fold_in(rng, 3), *heavy), -bound, bound).astype(kind)


def setup_inputs(seed: int = 0) -> dict:
    key_of = jax.random.split(jax.random.key(seed), 10)
    return {
        "goal_states": noise_with(key_of[0], (N_REP, GOALS_GRP, L, D), 1.0, 6.0, ((0, 4), (1, 8)), (1, 3, 8, 2.0)),
        "premise_states": noise_with(key_of[1], (N_REP, PREM_GRP, L, D), 1.0, 6.0, ((0, 4), (1, 8)), (1, 3, 8, 2.0)),
        "goal_ids": draw_goal_ids(jax.random.fold_in(key_of[9], 71), 0),
        "premise_ids": draw_premise_ids(jax.random.fold_in(key_of[9], 71), 0),
        "positives": set_ends(jax.random.randint(key_of[4], (N_REP, GOALS_GRP), 0, PREM_GRP), jax.random.fold_in(key_of[4], 1), 0, PREM_GRP - 1).astype(jnp.int32),
        "depthwise_kernels": gaussian(key_of[5], (2, K, D), K ** -0.5, 3.5, (), jnp.float32),
        "block_norm_gains": jnp.clip(1.0 + 0.15 * jax.random.normal(key_of[6], (2, D), jnp.float32), 0.25, 1.75),
        "pointwise_weights": gaussian(key_of[7], (2, D, D), D ** -0.5, 0.25),
        "head_weight": gaussian(key_of[8], (D, E), D ** -0.5, 0.25),
    }


logit_scale = 20.0

def shift_down(values, dilation):
    return jnp.pad(values, ((0, 0), (dilation, 0), (0, 0)))[:, :values.shape[1]]

def shift_up(values, dilation):
    return jnp.pad(values, ((0, 0), (0, dilation), (0, 0)))[:, dilation:]

def depth_conv(inputs, kernel, dilation):
    return kernel[0] * shift_down(inputs, dilation) + kernel[1] * inputs + kernel[2] * shift_up(inputs, dilation)

def conv_block_forward(hidden, kernel, gain, weight, token_valid_mask, dilation):
    widened = hidden.astype(jnp.float32)
    inverse = lax.rsqrt(lax.optimization_barrier(jnp.mean(widened * widened, axis=-1, keepdims=True)) + 1e-06)
    normed = widened * inverse * gain * token_valid_mask
    mixed = depth_conv(normed, kernel, dilation).astype(jnp.bfloat16)
    count, length, width = hidden.shape
    pre_act = jnp.dot(mixed.reshape(count * length, width), weight, preferred_element_type=jnp.float32).reshape(count, length, width)
    output = (widened + jax.nn.gelu(pre_act, approximate=True)).astype(jnp.bfloat16)
    return (output, (inverse, mixed, pre_act))

def conv_block_backward(upstream, hidden, saved, kernel, gain, weight, token_valid_mask, dilation, need_input):
    inverse, mixed, pre_act = saved
    widened = hidden.astype(jnp.float32)
    normed = widened * inverse * gain * token_valid_mask
    ignored_value, gelu_back = jax.vjp(lambda value: jax.nn.gelu(value, approximate=True), pre_act)
    act_grad = gelu_back(upstream)[0].astype(jnp.bfloat16)
    count, length, width = hidden.shape
    flat_grad = act_grad.reshape(count * length, width)
    grad_weight = jnp.dot(mixed.reshape(count * length, width).T, flat_grad, preferred_element_type=jnp.float32)
    conv_grad = jnp.dot(flat_grad, weight.T, preferred_element_type=jnp.float32).reshape(count, length, width)
    grad_kernel = jnp.stack([lax.optimization_barrier(jnp.sum(shift_down(normed, dilation) * conv_grad, axis=(0, 1))), lax.optimization_barrier(jnp.sum(normed * conv_grad, axis=(0, 1))), lax.optimization_barrier(jnp.sum(shift_up(normed, dilation) * conv_grad, axis=(0, 1)))])
    normed_grad = (kernel[0] * shift_up(conv_grad, dilation) + kernel[1] * conv_grad + kernel[2] * shift_down(conv_grad, dilation)) * token_valid_mask
    grad_gain = lax.optimization_barrier(jnp.sum(normed_grad * widened * inverse, axis=(0, 1)))
    input_grad = None
    if need_input:
        scaled = normed_grad * gain
        input_grad = upstream + inverse * scaled - widened * inverse ** 3 * lax.optimization_barrier(jnp.mean(scaled * widened, axis=-1, keepdims=True))
    return (input_grad, grad_kernel, grad_gain, grad_weight)

def pool_forward(hidden, token_valid_mask, head_weight):
    widened = hidden.astype(jnp.float32)
    counts = lax.optimization_barrier(jnp.sum(token_valid_mask, axis=1))
    pooled = (lax.optimization_barrier(jnp.sum(widened * token_valid_mask, axis=1)) / counts).astype(jnp.bfloat16)
    embedded = jnp.dot(pooled, head_weight, preferred_element_type=jnp.float32)
    magnitude = jnp.sqrt(lax.optimization_barrier(jnp.sum(embedded * embedded, axis=-1, keepdims=True)) + 1e-06)
    unit = embedded / magnitude
    return (unit.astype(jnp.bfloat16), (counts, pooled, unit, magnitude))

def pool_backward(unit_grad, saved, token_valid_mask, head_weight):
    counts, pooled, unit, magnitude = saved
    embed_grad = ((unit_grad - unit * lax.optimization_barrier(jnp.sum(unit * unit_grad, axis=-1, keepdims=True))) / magnitude).astype(jnp.bfloat16)
    grad_head = jnp.dot(pooled.T, embed_grad, preferred_element_type=jnp.float32)
    pooled_grad = jnp.dot(embed_grad, head_weight.T, preferred_element_type=jnp.float32)
    hidden_gradient = (pooled_grad / counts)[:, None, :] * token_valid_mask
    return (hidden_gradient, grad_head)

def encode(token_states, token_ids, depthwise_kernels, block_norm_gains, pointwise_weights, head_weight):
    token_valid_mask = (token_ids != 0).astype(jnp.float32)[..., None]
    first_hidden, lower_residuals = conv_block_forward(token_states, depthwise_kernels[0], block_norm_gains[0], pointwise_weights[0], token_valid_mask, LOWER_DILATION)
    second_hidden, upper_residuals = conv_block_forward(first_hidden, depthwise_kernels[1], block_norm_gains[1], pointwise_weights[1], token_valid_mask, UPPER_DILATION)
    unit_half, saved_pool = pool_forward(second_hidden, token_valid_mask, head_weight)
    return (unit_half, (token_valid_mask, first_hidden, lower_residuals, upper_residuals, saved_pool))

def device_grads(token_states, token_ids, unit_grad, depthwise_kernels, block_norm_gains, pointwise_weights, head_weight):
    unit_half, saved = encode(token_states, token_ids, depthwise_kernels, block_norm_gains, pointwise_weights, head_weight)
    token_valid_mask, first_hidden, lower_residuals, upper_residuals, saved_pool = saved
    hidden_gradient, grad_head = pool_backward(unit_grad, saved_pool, token_valid_mask, head_weight)
    lower_gradient, upper_kernel, upper_gain, upper_weight = conv_block_backward(hidden_gradient, first_hidden, upper_residuals, depthwise_kernels[1], block_norm_gains[1], pointwise_weights[1], token_valid_mask, UPPER_DILATION, True)
    ignored_value, lower_kernel, lower_gain, lower_weight = conv_block_backward(lower_gradient, token_states, lower_residuals, depthwise_kernels[0], block_norm_gains[0], pointwise_weights[0], token_valid_mask, LOWER_DILATION, False)
    return (jnp.stack([lower_kernel, upper_kernel]), jnp.stack([lower_gain, upper_gain]), jnp.stack([lower_weight, upper_weight]), grad_head)

def group_scores(goal_units, premise_units, positive):
    scores = logit_scale * lax.dot_general(goal_units, premise_units, (((1,), (1,)), ((), ())), preferred_element_type=jnp.float32)
    expon = jnp.exp(scores)
    total = lax.optimization_barrier(jnp.sum(expon, axis=1, keepdims=True))
    columns = jnp.arange(premise_units.shape[0], dtype=jnp.int32)
    onehot = (columns[None, :] == positive[:, None]).astype(jnp.float32)
    losses = jnp.log(total[:, 0]) - lax.optimization_barrier(jnp.sum(scores * onehot, axis=1))
    score_grad = ((expon / total - onehot) / G_DEV).astype(jnp.bfloat16)
    goal_grad = logit_scale * jnp.dot(score_grad, premise_units, preferred_element_type=jnp.float32)
    premise_grad = logit_scale * lax.dot_general(score_grad, goal_units, (((0,), (0,)), ((), ())), preferred_element_type=jnp.float32)
    return (losses, goal_grad, premise_grad)

def reference(goal_states, premise_states, goal_ids, premise_ids, positives, depthwise_kernels, block_norm_gains, pointwise_weights, head_weight):
    devices = N_REP * N_NEG
    token_states = jnp.concatenate([goal_states.reshape(devices, G_DEV, L, D), premise_states.reshape(devices, P_DEV, L, D)], axis=1)
    token_ids = jnp.concatenate([goal_ids.reshape(devices, G_DEV, L), premise_ids.reshape(devices, P_DEV, L)], axis=1)

    def forward_one(pair):
        return encode(pair[0], pair[1], depthwise_kernels, block_norm_gains, pointwise_weights, head_weight)[0]
    units = lax.map(forward_one, (token_states, token_ids))
    goal_units = units[:, :G_DEV].reshape(N_REP, GOALS_GRP, E)
    premise_units = units[:, G_DEV:].reshape(N_REP, PREM_GRP, E)
    losses, goal_grads, premise_grads = lax.map(lambda triple: group_scores(triple[0], triple[1], triple[2]), (goal_units, premise_units, positives))
    unit_grads = jnp.concatenate([goal_grads.reshape(devices, G_DEV, E), premise_grads.reshape(devices, P_DEV, E)], axis=1)
    initial = (jnp.zeros((2, K, D), jnp.float32), jnp.zeros((2, D), jnp.float32), jnp.zeros((2, D, D), jnp.float32), jnp.zeros((D, E), jnp.float32))

    def accumulate(totals, triple):
        terms = device_grads(triple[0], triple[1], triple[2], depthwise_kernels, block_norm_gains, pointwise_weights, head_weight)
        return (jax.tree.map(jnp.add, totals, terms), None)
    totals, ignored_value = lax.scan(accumulate, initial, (token_states, token_ids, unit_grads))
    return (losses, totals[0], totals[1], totals[2], totals[3])
```

```python
import functools

import jax
import jax.numpy as jnp
from jax import lax
from jax.experimental import pallas as pl
from jax.experimental.pallas import tpu as pltpu
from jax.sharding import PartitionSpec as P

LOWER_DILATION = 4
UPPER_DILATION = 8
LOGIT_SCALE = 20.0
GELU_C = 0.7978845608028654
GELU_A = 0.044715
SEQS = 4
MESH = pl.DeviceIdType.MESH
VMEM_LIMIT = 56 * 1024 * 1024


def shift_down(values, dilation):
    zeros = jnp.zeros_like(values[:, :dilation])
    return jnp.concatenate([zeros, values[:, : values.shape[1] - dilation]], axis=1)


def shift_up(values, dilation):
    zeros = jnp.zeros_like(values[:, :dilation])
    return jnp.concatenate([values[:, dilation:], zeros], axis=1)


def gelu_and_slope(value):
    square = value * value
    half = 0.5 + 0.5 * jnp.tanh(value * (GELU_C + (GELU_C * GELU_A) * square))
    slope = half + value * (half - half * half) * (2.0 * GELU_C + (6.0 * GELU_C * GELU_A) * square)
    return value * half, slope


def length_mask(lens_ref, step, length):
    place = lax.broadcasted_iota(jnp.int32, (length, 1), 0)
    return jnp.stack(
        [(place < lens_ref[step * SEQS + s]).astype(jnp.float32) for s in range(SEQS)]
    )


def forward_kernel(
    goal_steps, lens_ref, goal_ref, prem_ref, kern_ref, gain_ref, weight_ref,
    n0_ref, m0_ref, d0_ref, n1_ref, m1_ref, d1_ref, inv_ref, pool_ref,
):
    step = pl.program_id(0)
    count, length, width = prem_ref.shape
    states = jnp.where(step < goal_steps, goal_ref[...], prem_ref[...])
    mask = length_mask(lens_ref, step, length)

    def block(hidden, b, dilation, n_ref, m_ref, d_ref):
        inverse = lax.rsqrt(jnp.mean(hidden * hidden, axis=-1, keepdims=True) + 1e-06) * mask
        unscaled = hidden * inverse
        n_ref[...] = unscaled.astype(jnp.bfloat16)
        taps = kern_ref[b] * gain_ref[b][None, :]
        mixed = (
            taps[0] * shift_down(unscaled, dilation)
            + taps[1] * unscaled
            + taps[2] * shift_up(unscaled, dilation)
        ).astype(jnp.bfloat16)
        m_ref[...] = mixed
        pre_act = jnp.dot(
            mixed.reshape(count * length, width), weight_ref[b], preferred_element_type=jnp.float32
        ).reshape(count, length, width)
        act, slope = gelu_and_slope(pre_act)
        d_ref[...] = slope.astype(jnp.bfloat16)
        return (hidden + act).astype(jnp.bfloat16), inverse

    first, _ = block(states.astype(jnp.float32), 0, LOWER_DILATION, n0_ref, m0_ref, d0_ref)
    second, inverse = block(first.astype(jnp.float32), 1, UPPER_DILATION, n1_ref, m1_ref, d1_ref)
    inv_ref[...] = jnp.broadcast_to(inverse, inv_ref.shape)
    row = lax.broadcasted_iota(jnp.int32, (8, count * length), 0)
    col = lax.broadcasted_iota(jnp.int32, (8, count * length), 1)
    picks = jnp.zeros((8, count * length), jnp.float32)
    for s in range(SEQS):
        own = (row == s) & (col >= s * length) & (col < s * length + lens_ref[step * SEQS + s])
        picks = jnp.where(own, 1.0, picks)
    pool_ref[...] = jnp.dot(
        picks.astype(jnp.bfloat16),
        second.reshape(count * length, width),
        preferred_element_type=jnp.float32,
    )[None]


def run_forward(lens, goals, premises, kernels, gains, weights):
    goal_count, length, width = goals.shape
    goal_steps = goal_count // SEQS
    total = goal_count + premises.shape[0]
    steps = total // SEQS
    block = pl.BlockSpec((SEQS, length, width), lambda i, lens: (i, 0, 0))
    whole = lambda shape: pl.BlockSpec(shape, lambda i, lens: (0,) * len(shape))
    state = jax.ShapeDtypeStruct((total, length, width), jnp.bfloat16)
    return pl.pallas_call(
        functools.partial(forward_kernel, goal_steps),
        grid_spec=pltpu.PrefetchScalarGridSpec(
            num_scalar_prefetch=1,
            grid=(steps,),
            in_specs=[
                pl.BlockSpec(
                    (SEQS, length, width), lambda i, lens: (jnp.minimum(i, goal_steps - 1), 0, 0)
                ),
                pl.BlockSpec(
                    (SEQS, length, width), lambda i, lens: (jnp.maximum(i - goal_steps, 0), 0, 0)
                ),
                whole(kernels.shape),
                whole(gains.shape),
                whole(weights.shape),
            ],
            out_specs=[block] * 6
            + [
                pl.BlockSpec((SEQS, length, 128), lambda i, lens: (i, 0, 0)),
                pl.BlockSpec((1, 8, width), lambda i, lens: (i, 0, 0)),
            ],
        ),
        out_shape=[state] * 6
        + [
            jax.ShapeDtypeStruct((total, length, 128), jnp.float32),
            jax.ShapeDtypeStruct((steps, 8, width), jnp.float32),
        ],
        compiler_params=pltpu.CompilerParams(vmem_limit_bytes=VMEM_LIMIT),
    )(lens, goals, premises, kernels, gains, weights)


def contrast_kernel(
    n_neg, goal_count, pooled_ref, lens_ref, head_ref, positive_ref,
    loss_ref, pooled_grad_ref, head_grad_ref,
    units_ref, loss_all, goal_all, prem_all, send_sem, recv_sem,
):
    me = lax.axis_index("neg")
    barrier = pltpu.get_barrier_semaphore()

    @pl.loop(1, n_neg)
    def _(k):
        pl.semaphore_signal(
            barrier, inc=1, device_id={"neg": lax.rem(me + k, n_neg)}, device_id_type=MESH
        )

    rows = pooled_ref.shape[0]
    lens = lens_ref[...]
    pooled = (pooled_ref[...] / lens).astype(jnp.bfloat16)
    head = head_ref[...]
    embedded = jnp.dot(pooled, head, preferred_element_type=jnp.float32)
    magnitude = jnp.sqrt(jnp.sum(embedded * embedded, axis=-1, keepdims=True) + 1e-06)
    unit = embedded / magnitude
    units_ref[me] = unit.astype(jnp.bfloat16)
    pl.semaphore_wait(barrier, n_neg - 1)

    def copy_to(k):
        peer = lax.rem(me + k, n_neg)
        return pltpu.make_async_remote_copy(
            src_ref=units_ref.at[me],
            dst_ref=units_ref.at[me],
            send_sem=send_sem.at[k],
            recv_sem=recv_sem.at[me],
            device_id={"neg": peer},
            device_id_type=MESH,
        )

    @pl.loop(1, n_neg)
    def _(k):
        copy_to(k).start()

    @pl.loop(1, n_neg)
    def _(k):
        source = lax.rem(me + k, n_neg)
        pltpu.make_async_remote_copy(
            src_ref=units_ref.at[source],
            dst_ref=units_ref.at[source],
            send_sem=send_sem.at[k],
            recv_sem=recv_sem.at[source],
            device_id={"neg": source},
            device_id_type=MESH,
        ).wait_recv()

    everyone = units_ref[...].astype(jnp.float32)
    width = everyone.shape[-1]
    prem_count = rows - 2 * goal_count
    goals = everyone[:, :goal_count].reshape(n_neg * goal_count, width).astype(jnp.bfloat16)
    premises = everyone[:, 2 * goal_count :].reshape(n_neg * prem_count, width).astype(jnp.bfloat16)
    scores = LOGIT_SCALE * lax.dot_general(
        goals, premises, (((1,), (1,)), ((), ())), preferred_element_type=jnp.float32
    )
    expon = jnp.exp(scores)
    total = jnp.sum(expon, axis=1, keepdims=True)
    columns = lax.broadcasted_iota(jnp.int32, scores.shape, 1)
    onehot = (columns == positive_ref[...]).astype(jnp.float32)
    loss = jnp.log(total) - jnp.sum(scores * onehot, axis=1, keepdims=True)
    loss_all[...] = jnp.broadcast_to(loss, loss_all.shape)
    score_grad = ((expon / total - onehot) / goal_count).astype(jnp.bfloat16)
    goal_all[...] = LOGIT_SCALE * jnp.dot(score_grad, premises, preferred_element_type=jnp.float32)
    prem_all[...] = LOGIT_SCALE * lax.dot_general(
        score_grad, goals, (((0,), (0,)), ((), ())), preferred_element_type=jnp.float32
    )
    own_goals = pl.ds(pl.multiple_of(me * goal_count, goal_count), goal_count)
    own_prems = pl.ds(pl.multiple_of(me * prem_count, prem_count), prem_count)
    loss_ref[...] = loss_all[own_goals, :]
    own_goal_grad = goal_all[own_goals, :]
    unit_grad = jnp.concatenate(
        [own_goal_grad, jnp.zeros_like(own_goal_grad), prem_all[own_prems, :]], axis=0
    )
    embed_grad = (
        (unit_grad - unit * jnp.sum(unit * unit_grad, axis=-1, keepdims=True)) / magnitude
    ).astype(jnp.bfloat16)
    head_grad_ref[...] = lax.dot_general(
        pooled, embed_grad, (((0,), (0,)), ((), ())), preferred_element_type=jnp.float32
    )
    pooled_grad = lax.dot_general(
        embed_grad, head, (((1,), (1,)), ((), ())), preferred_element_type=jnp.float32
    )
    pooled_grad_ref[...] = pooled_grad / lens

    @pl.loop(1, n_neg)
    def _(k):
        copy_to(k).wait_send()


def run_contrast(n_neg, goal_count, pooled, lens, head, positives):
    rows, width = pooled.shape
    embed = head.shape[1]
    prem_count = rows - 2 * goal_count
    vmem = pl.BlockSpec(memory_space=pltpu.VMEM)
    return pl.pallas_call(
        functools.partial(contrast_kernel, n_neg, goal_count),
        out_shape=[
            jax.ShapeDtypeStruct((goal_count, 128), jnp.float32),
            jax.ShapeDtypeStruct((rows, width), jnp.float32),
            jax.ShapeDtypeStruct((width, embed), jnp.float32),
        ],
        in_specs=[vmem] * 4,
        out_specs=[vmem] * 3,
        scratch_shapes=[
            pltpu.VMEM((n_neg, rows, embed), jnp.bfloat16),
            pltpu.VMEM((n_neg * goal_count, 128), jnp.float32),
            pltpu.VMEM((n_neg * goal_count, embed), jnp.float32),
            pltpu.VMEM((n_neg * prem_count, embed), jnp.float32),
            pltpu.SemaphoreType.DMA((n_neg,)),
            pltpu.SemaphoreType.DMA((n_neg,)),
        ],
        compiler_params=pltpu.CompilerParams(
            collective_id=0, has_side_effects=True, vmem_limit_bytes=VMEM_LIMIT
        ),
    )(pooled, lens, head, positives)


def backward_kernel(
    lens_ref, n0_ref, m0_ref, d0_ref, n1_ref, m1_ref, d1_ref, inv_ref, up_ref,
    kern_ref, gain_ref, weight_ref,
    point_ref, small_ref, sums_ref,
):
    step = pl.program_id(0)
    count, length, width = n0_ref.shape
    tokens = count * length

    @pl.when(step == 0)
    def _():
        point_ref[...] = jnp.zeros_like(point_ref)
        sums_ref[...] = jnp.zeros_like(sums_ref)

    def fold(values):
        return jnp.sum(values.reshape(tokens // 8, 8, width), axis=0)

    def block(upstream, b, dilation, m_ref, d_ref, unscaled, need_input):
        act_grad = (upstream * d_ref[...].astype(jnp.float32)).astype(jnp.bfloat16)
        flat = act_grad.reshape(tokens, width)
        point_ref[b] += lax.dot_general(
            m_ref[...].reshape(tokens, width),
            flat,
            (((0,), (0,)), ((), ())),
            preferred_element_type=jnp.float32,
        )
        conv = lax.dot_general(
            flat, weight_ref[b], (((1,), (1,)), ((), ())), preferred_element_type=jnp.float32
        ).reshape(count, length, width)
        above = shift_up(conv, dilation)
        below = shift_down(conv, dilation)
        sums_ref[b, 0] += fold(above * unscaled)
        sums_ref[b, 1] += fold(conv * unscaled)
        sums_ref[b, 2] += fold(below * unscaled)
        if not need_input:
            return None
        taps = kern_ref[b] * gain_ref[b][None, :]
        scaled = taps[0] * above + taps[1] * conv + taps[2] * below
        mean = jnp.mean(scaled * unscaled, axis=-1, keepdims=True)
        inverse = inv_ref[:, :, :1]
        return upstream + inverse * (scaled - unscaled * mean)

    mask = length_mask(lens_ref, step, length)
    upstream = up_ref[...] * mask
    lower = block(
        upstream, 1, UPPER_DILATION, m1_ref, d1_ref, n1_ref[...].astype(jnp.float32), True
    )
    block(lower, 0, LOWER_DILATION, m0_ref, d0_ref, n0_ref[...].astype(jnp.float32), False)

    @pl.when(step == pl.num_programs(0) - 1)
    def _():
        rows = []
        for b in range(2):
            plain = jnp.sum(sums_ref[b], axis=1)
            rows.append(plain * gain_ref[b][None, :])
            rows.append(jnp.sum(plain * kern_ref[b], axis=0, keepdims=True))
        small_ref[...] = jnp.concatenate([rows[0], rows[2], rows[1], rows[3]], axis=0)


def run_backward(lens, saved, pooled_grad, kernels, gains, weights):
    total, length, width = saved[0].shape
    steps = total // SEQS
    block = pl.BlockSpec((SEQS, length, width), lambda i, lens: (i, 0, 0))
    whole = lambda shape: pl.BlockSpec(shape, lambda i, lens: (0,) * len(shape))
    return pl.pallas_call(
        backward_kernel,
        grid_spec=pltpu.PrefetchScalarGridSpec(
            num_scalar_prefetch=1,
            grid=(steps,),
            in_specs=[block] * 6
            + [
                pl.BlockSpec((SEQS, length, 128), lambda i, lens: (i, 0, 0)),
                pl.BlockSpec((SEQS, 1, width), lambda i, lens: (i, 0, 0)),
                whole(kernels.shape),
                whole(gains.shape),
                whole(weights.shape),
            ],
            out_specs=[whole(weights.shape), whole((8, width))],
            scratch_shapes=[pltpu.VMEM((2, 3, 8, width), jnp.float32)],
        ),
        out_shape=[
            jax.ShapeDtypeStruct(weights.shape, jnp.float32),
            jax.ShapeDtypeStruct((8, width), jnp.float32),
        ],
        compiler_params=pltpu.CompilerParams(vmem_limit_bytes=VMEM_LIMIT),
    )(lens, *saved, pooled_grad, kernels, gains, weights)


def reduce_kernel(
    n_neg, n_rep, point_ref, head_ref, small_ref,
    point_out, head_out, small_out,
    mine_ref, pair_ref, slots_ref, full_ref,
    pair_send, pair_recv, send_sem, recv_sem, send2_sem, recv2_sem, last_send, last_recv,
):
    neg = lax.axis_index("neg")
    rep = lax.axis_index("rep")
    half_rep = n_rep // 2
    chips = n_neg * half_rep
    core = lax.rem(rep, 2)
    other = 1 - core
    me = neg * half_rep + rep // 2
    twin = {"neg": neg, "rep": rep + 1 - 2 * core}

    def device_of(chip):
        return {"neg": chip // half_rep, "rep": 2 * lax.rem(chip, half_rep) + core}

    barrier = pltpu.get_barrier_semaphore()
    pl.semaphore_signal(barrier, inc=1, device_id=twin, device_id_type=MESH)

    @pl.loop(1, chips)
    def _(k):
        pl.semaphore_signal(
            barrier, inc=1, device_id=device_of(lax.rem(me + k, chips)), device_id_type=MESH
        )

    width = point_ref.shape[-1]
    cols = width // 2
    point_rows = 2 * width
    head_rows = head_ref.shape[0] // 2
    small_row = point_rows + head_rows
    total = mine_ref.shape[1]
    share = total // chips
    for h in range(2):
        side = slice(h * cols, (h + 1) * cols)
        for b in range(2):
            mine_ref[h, b * width : (b + 1) * width] = point_ref[b, :, side].astype(jnp.bfloat16)
        mine_ref[h, point_rows:small_row] = head_ref[
            h * head_rows : (h + 1) * head_rows, :
        ].astype(jnp.bfloat16)
        mine_ref[h, small_row:] = jnp.concatenate(
            [small_ref[:, side], jnp.zeros((total - small_row - 8, cols), jnp.float32)], axis=0
        ).astype(jnp.bfloat16)
    pl.semaphore_wait(barrier, chips)

    pair = pltpu.make_async_remote_copy(
        src_ref=mine_ref.at[other],
        dst_ref=pair_ref,
        send_sem=pair_send,
        recv_sem=pair_recv,
        device_id=twin,
        device_id_type=MESH,
    )
    pair.start()
    pair.wait_recv()
    mine_ref[core] = (
        mine_ref[core].astype(jnp.float32) + pair_ref[...].astype(jnp.float32)
    ).astype(jnp.bfloat16)

    def rows_of(chip):
        return pl.ds(pl.multiple_of(chip * share, 16), share)

    def scatter(k):
        chip = lax.rem(me + k, chips)
        return pltpu.make_async_remote_copy(
            src_ref=mine_ref.at[core, rows_of(chip)],
            dst_ref=slots_ref.at[me],
            send_sem=send_sem.at[k],
            recv_sem=recv_sem.at[me],
            device_id=device_of(chip),
            device_id_type=MESH,
        )

    def scattered(k):
        chip = lax.rem(me + k, chips)
        return pltpu.make_async_remote_copy(
            src_ref=slots_ref.at[chip],
            dst_ref=slots_ref.at[chip],
            send_sem=send_sem.at[k],
            recv_sem=recv_sem.at[chip],
            device_id=device_of(chip),
            device_id_type=MESH,
        )

    @pl.loop(1, chips)
    def _(k):
        scatter(k).start()

    slots_ref[me] = mine_ref[core, rows_of(me)]

    @pl.loop(1, chips)
    def _(k):
        scattered(k).wait_recv()

    reduced = lax.fori_loop(
        0,
        chips,
        lambda c, acc: acc + slots_ref[c].astype(jnp.float32),
        jnp.zeros((share, cols), jnp.float32),
    )
    full_ref[core, rows_of(me)] = reduced.astype(jnp.bfloat16)

    def gather(k, chip):
        return pltpu.make_async_remote_copy(
            src_ref=full_ref.at[core, rows_of(chip)],
            dst_ref=full_ref.at[core, rows_of(chip)],
            send_sem=send2_sem.at[k],
            recv_sem=recv2_sem.at[chip],
            device_id=device_of(lax.rem(me + k, chips)),
            device_id_type=MESH,
        )

    def forward(chip):
        return pltpu.make_async_remote_copy(
            src_ref=full_ref.at[core, rows_of(chip)],
            dst_ref=full_ref.at[core, rows_of(chip)],
            send_sem=last_send.at[chip],
            recv_sem=last_recv.at[chip],
            device_id=twin,
            device_id_type=MESH,
        )

    def forwarded(chip):
        return pltpu.make_async_remote_copy(
            src_ref=full_ref.at[other, rows_of(chip)],
            dst_ref=full_ref.at[other, rows_of(chip)],
            send_sem=last_send.at[chip],
            recv_sem=last_recv.at[chip],
            device_id=twin,
            device_id_type=MESH,
        )

    @pl.loop(1, chips)
    def _(k):
        gather(k, me).start()

    forward(me).start()

    @pl.loop(1, chips)
    def _(k):
        chip = lax.rem(me + k, chips)
        gather(k, chip).wait_recv()
        forward(chip).start()

    @pl.loop(0, chips)
    def _(chip):
        forwarded(chip).wait_recv()

    for h in range(2):
        side = slice(h * cols, (h + 1) * cols)
        for b in range(2):
            point_out[b, :, side] = full_ref[h, b * width : (b + 1) * width].astype(jnp.float32)
        head_out[h * head_rows : (h + 1) * head_rows, :] = full_ref[
            h, point_rows:small_row
        ].astype(jnp.float32)
        small_out[:, side] = full_ref[h, small_row : small_row + 16].astype(jnp.float32)[:8]

    pair.wait_send()

    @pl.loop(1, chips)
    def _(k):
        scatter(k).wait_send()
        gather(k, me).wait_send()

    @pl.loop(0, chips)
    def _(chip):
        forward(chip).wait_send()


def run_reduce(n_neg, n_rep, point, head, small):
    chips = n_neg * n_rep // 2
    width = point.shape[-1]
    cols = width // 2
    grain = 16 * chips
    used = 2 * width + head.shape[0] // 2 + 16
    total = -(-used // grain) * grain
    vmem = pl.BlockSpec(memory_space=pltpu.VMEM)
    dma = pltpu.SemaphoreType.DMA
    return pl.pallas_call(
        functools.partial(reduce_kernel, n_neg, n_rep),
        out_shape=[
            jax.ShapeDtypeStruct(point.shape, jnp.float32),
            jax.ShapeDtypeStruct(head.shape, jnp.float32),
            jax.ShapeDtypeStruct(small.shape, jnp.float32),
        ],
        in_specs=[vmem] * 3,
        out_specs=[vmem] * 3,
        scratch_shapes=[
            pltpu.VMEM((2, total, cols), jnp.bfloat16),
            pltpu.VMEM((total, cols), jnp.bfloat16),
            pltpu.VMEM((chips, total // chips, cols), jnp.bfloat16),
            pltpu.VMEM((2, total, cols), jnp.bfloat16),
            dma, dma,
            dma((chips,)), dma((chips,)), dma((chips,)), dma((chips,)),
            dma((chips,)), dma((chips,)),
        ],
        compiler_params=pltpu.CompilerParams(
            collective_id=1, has_side_effects=True, vmem_limit_bytes=VMEM_LIMIT
        ),
    )(point, head, small)


def local(
    n_neg,
    n_rep,
    goal_states,
    premise_states,
    goal_ids,
    premise_ids,
    positives,
    kernels,
    gains,
    weights,
    head_weight,
):
    goals, premises = goal_states[0], premise_states[0]
    goal_count, length, width = goals.shape
    total = goal_count + premises.shape[0]
    ids = jnp.concatenate([goal_ids[0], premise_ids[0]], axis=0)
    lens = jnp.sum((ids != 0).astype(jnp.int32), axis=1)
    *saved, pool_sums = run_forward(lens, goals, premises, kernels, gains, weights)

    def widen(rows, fill):
        gap = jnp.full((goal_count, rows.shape[1]), fill, rows.dtype)
        return jnp.concatenate([rows[:goal_count], gap, rows[goal_count:]], axis=0)

    pooled = widen(pool_sums[:, :SEQS].reshape(total, width), 0.0)
    spans = widen(lens.astype(jnp.float32)[:, None], 1.0)
    loss, pooled_grad, head_grad = run_contrast(
        n_neg, goal_count, pooled, spans, head_weight, positives.reshape(-1, 1)
    )
    upstream = jnp.concatenate([pooled_grad[:goal_count], pooled_grad[2 * goal_count :]], axis=0)
    point, small = run_backward(lens, saved, upstream[:, None, :], kernels, gains, weights)
    point, head, small = run_reduce(n_neg, n_rep, point, head_grad, small)
    return (
        loss[:, 0][None, :],
        small[:6].reshape(2, 3, width),
        small[6:],
        point,
        head,
    )


def solution(mesh):
    placed = (
        P("rep", "neg", None, None),
        P("rep", "neg", None, None),
        P("rep", "neg", None),
        P("rep", "neg", None),
        P("rep", None),
        P(),
        P(),
        P(),
        P(),
    )
    return jax.shard_map(
        functools.partial(local, mesh.shape["neg"], mesh.shape["rep"]),
        mesh=mesh,
        in_specs=placed,
        out_specs=(P("rep", "neg"), P(), P(), P(), P()),
        check_vma=False,
    )
```

```python
import functools

import jax
import jax.numpy as jnp
from jax import lax
from jax.experimental import pallas as pl
from jax.experimental.pallas import tpu as pltpu
from jax.sharding import PartitionSpec as P

LOWER_DILATION = 4
UPPER_DILATION = 8
LOGIT_SCALE = 20.0
GELU_C = 0.7978845608028654
GELU_A = 0.044715
SEQS = 4
MESH = pl.DeviceIdType.MESH
VMEM_LIMIT = 56 * 1024 * 1024


def shift_down(values, dilation):
    zeros = jnp.zeros_like(values[:, :dilation])
    return jnp.concatenate([zeros, values[:, : values.shape[1] - dilation]], axis=1)


def shift_up(values, dilation):
    zeros = jnp.zeros_like(values[:, :dilation])
    return jnp.concatenate([values[:, dilation:], zeros], axis=1)


def gelu_and_slope(value):
    square = value * value
    half = 0.5 + 0.5 * jnp.tanh(value * (GELU_C + (GELU_C * GELU_A) * square))
    slope = half + value * (half - half * half) * (2.0 * GELU_C + (6.0 * GELU_C * GELU_A) * square)
    return value * half, slope


def length_mask(lens_ref, step, length):
    place = lax.broadcasted_iota(jnp.int32, (length, 1), 0)
    return jnp.stack(
        [(place < lens_ref[step * SEQS + s]).astype(jnp.float32) for s in range(SEQS)]
    )


def length_column(lens_ref, step):
    row = lax.broadcasted_iota(jnp.int32, (8, 1), 0)
    spans = jnp.ones((8, 1), jnp.float32)
    for s in range(SEQS):
        spans = jnp.where(row == s, lens_ref[step * SEQS + s].astype(jnp.float32), spans)
    return spans


def forward_kernel(
    goal_steps, lens_ref, goal_ref, prem_ref, kern_ref, gain_ref, weight_ref,
    n0_ref, m0_ref, d0_ref, n1_ref, m1_ref, d1_ref, inv_ref, pool_ref,
):
    step = pl.program_id(0)
    count, length, width = prem_ref.shape
    states = jnp.where(step < goal_steps, goal_ref[...], prem_ref[...])
    mask = length_mask(lens_ref, step, length)

    def block(hidden, b, dilation, n_ref, m_ref, d_ref):
        inverse = lax.rsqrt(jnp.mean(hidden * hidden, axis=-1, keepdims=True) + 1e-06) * mask
        unscaled = hidden * inverse
        n_ref[...] = unscaled.astype(jnp.bfloat16)
        taps = kern_ref[b] * gain_ref[b][None, :]
        mixed = (
            taps[0] * shift_down(unscaled, dilation)
            + taps[1] * unscaled
            + taps[2] * shift_up(unscaled, dilation)
        ).astype(jnp.bfloat16)
        m_ref[...] = mixed
        pre_act = jnp.dot(
            mixed.reshape(count * length, width), weight_ref[b], preferred_element_type=jnp.float32
        ).reshape(count, length, width)
        act, slope = gelu_and_slope(pre_act)
        d_ref[...] = slope.astype(jnp.bfloat16)
        return (hidden + act).astype(jnp.bfloat16), inverse

    first, _ = block(states.astype(jnp.float32), 0, LOWER_DILATION, n0_ref, m0_ref, d0_ref)
    second, inverse = block(first.astype(jnp.float32), 1, UPPER_DILATION, n1_ref, m1_ref, d1_ref)
    inv_ref[...] = jnp.broadcast_to(inverse, inv_ref.shape)
    row = lax.broadcasted_iota(jnp.int32, (8, count * length), 0)
    col = lax.broadcasted_iota(jnp.int32, (8, count * length), 1)
    picks = jnp.zeros((8, count * length), jnp.float32)
    for s in range(SEQS):
        own = (row == s) & (col >= s * length) & (col < s * length + lens_ref[step * SEQS + s])
        picks = jnp.where(own, 1.0, picks)
    sums = jnp.dot(
        picks.astype(jnp.bfloat16),
        second.reshape(count * length, width),
        preferred_element_type=jnp.float32,
    )
    pool_ref[...] = (sums / length_column(lens_ref, step))[None]


def run_forward(lens, goals, premises, kernels, gains, weights):
    goal_count, length, width = goals.shape
    goal_steps = goal_count // SEQS
    total = goal_count + premises.shape[0]
    steps = total // SEQS
    block = pl.BlockSpec((SEQS, length, width), lambda i, lens: (i, 0, 0))
    whole = lambda shape: pl.BlockSpec(shape, lambda i, lens: (0,) * len(shape))
    state = jax.ShapeDtypeStruct((total, length, width), jnp.bfloat16)
    return pl.pallas_call(
        functools.partial(forward_kernel, goal_steps),
        grid_spec=pltpu.PrefetchScalarGridSpec(
            num_scalar_prefetch=1,
            grid=(steps,),
            in_specs=[
                pl.BlockSpec(
                    (SEQS, length, width), lambda i, lens: (jnp.minimum(i, goal_steps - 1), 0, 0)
                ),
                pl.BlockSpec(
                    (SEQS, length, width), lambda i, lens: (jnp.maximum(i - goal_steps, 0), 0, 0)
                ),
                whole(kernels.shape),
                whole(gains.shape),
                whole(weights.shape),
            ],
            out_specs=[block] * 6
            + [
                pl.BlockSpec((SEQS, length, 128), lambda i, lens: (i, 0, 0)),
                pl.BlockSpec((1, 8, width), lambda i, lens: (i, 0, 0)),
            ],
        ),
        out_shape=[state] * 6
        + [
            jax.ShapeDtypeStruct((total, length, 128), jnp.float32),
            jax.ShapeDtypeStruct((steps, 8, width), jnp.float32),
        ],
        compiler_params=pltpu.CompilerParams(vmem_limit_bytes=VMEM_LIMIT),
    )(lens, goals, premises, kernels, gains, weights)


def contrast_kernel(
    n_neg, goal_count, pooled_ref, head_ref, positive_ref,
    loss_ref, pooled_grad_ref, head_grad_ref,
    units_ref, goal_all, prem_all, send_sem, recv_sem,
):
    me = lax.axis_index("neg")
    barrier = pltpu.get_barrier_semaphore()

    @pl.loop(1, n_neg)
    def _(k):
        pl.semaphore_signal(
            barrier, inc=1, device_id={"neg": lax.rem(me + k, n_neg)}, device_id_type=MESH
        )

    steps, _, width = pooled_ref.shape
    goal_steps = goal_count // SEQS
    prem_count = steps * SEQS - goal_count
    pieces = [pooled_ref[i, :SEQS] for i in range(steps)]
    gap = jnp.zeros((goal_count, width), jnp.float32)
    pooled = jnp.concatenate(pieces[:goal_steps] + [gap] + pieces[goal_steps:], axis=0).astype(
        jnp.bfloat16
    )
    head = head_ref[...]
    embedded = jnp.dot(pooled, head, preferred_element_type=jnp.float32)
    magnitude = jnp.sqrt(jnp.sum(embedded * embedded, axis=-1, keepdims=True) + 1e-06)
    unit = embedded / magnitude
    units_ref[me] = unit.astype(jnp.bfloat16)
    pl.semaphore_wait(barrier, n_neg - 1)

    def copy_to(k):
        peer = lax.rem(me + k, n_neg)
        return pltpu.make_async_remote_copy(
            src_ref=units_ref.at[me],
            dst_ref=units_ref.at[me],
            send_sem=send_sem.at[k],
            recv_sem=recv_sem.at[me],
            device_id={"neg": peer},
            device_id_type=MESH,
        )

    @pl.loop(1, n_neg)
    def _(k):
        copy_to(k).start()

    @pl.loop(1, n_neg)
    def _(k):
        source = lax.rem(me + k, n_neg)
        pltpu.make_async_remote_copy(
            src_ref=units_ref.at[source],
            dst_ref=units_ref.at[source],
            send_sem=send_sem.at[k],
            recv_sem=recv_sem.at[source],
            device_id={"neg": source},
            device_id_type=MESH,
        ).wait_recv()

    everyone = units_ref[...].astype(jnp.float32)
    embed = everyone.shape[-1]
    goals = everyone[:, :goal_count].reshape(n_neg * goal_count, embed).astype(jnp.bfloat16)
    premises = everyone[:, 2 * goal_count :].reshape(n_neg * prem_count, embed).astype(jnp.bfloat16)
    scores = LOGIT_SCALE * lax.dot_general(
        premises, goals, (((1,), (1,)), ((), ())), preferred_element_type=jnp.float32
    )
    expon = jnp.exp(scores)
    total = jnp.sum(expon, axis=0, keepdims=True)
    places = lax.broadcasted_iota(jnp.int32, scores.shape, 0)
    onehot = (places == positive_ref[...]).astype(jnp.float32)
    loss = jnp.log(total) - jnp.sum(scores * onehot, axis=0, keepdims=True)
    group = (n_neg * goal_count, goal_count)
    pick = (
        lax.broadcasted_iota(jnp.int32, group, 0)
        == me * goal_count + lax.broadcasted_iota(jnp.int32, group, 1)
    ).astype(jnp.float32)
    loss_ref[...] = jnp.dot(
        jnp.broadcast_to(loss, (8, loss.shape[1])),
        pick,
        precision=lax.Precision.HIGHEST,
        preferred_element_type=jnp.float32,
    )[:1]
    score_grad = ((expon / total - onehot) / goal_count).astype(jnp.bfloat16)
    goal_all[...] = LOGIT_SCALE * lax.dot_general(
        score_grad, premises, (((0,), (0,)), ((), ())), preferred_element_type=jnp.float32
    )
    prem_all[...] = LOGIT_SCALE * jnp.dot(score_grad, goals, preferred_element_type=jnp.float32)
    own_goals = pl.ds(pl.multiple_of(me * goal_count, goal_count), goal_count)
    own_prems = pl.ds(pl.multiple_of(me * prem_count, prem_count), prem_count)
    own_goal_grad = goal_all[own_goals, :]
    unit_grad = jnp.concatenate(
        [own_goal_grad, jnp.zeros_like(own_goal_grad), prem_all[own_prems, :]], axis=0
    )
    embed_grad = (
        (unit_grad - unit * jnp.sum(unit * unit_grad, axis=-1, keepdims=True)) / magnitude
    ).astype(jnp.bfloat16)
    head_grad = lax.dot_general(
        pooled, embed_grad, (((0,), (0,)), ((), ())), preferred_element_type=jnp.float32
    )
    head_grad_ref[...] = head_grad.astype(jnp.bfloat16).reshape(head_grad_ref.shape)
    pooled_grad = lax.dot_general(
        embed_grad, head, (((1,), (1,)), ((), ())), preferred_element_type=jnp.float32
    )
    for i in range(steps):
        start = i * SEQS + (goal_count if i >= goal_steps else 0)
        pooled_grad_ref[i, :SEQS] = pooled_grad[start : start + SEQS]
        pooled_grad_ref[i, SEQS:] = jnp.zeros((8 - SEQS, width), jnp.float32)

    @pl.loop(1, n_neg)
    def _(k):
        copy_to(k).wait_send()


def run_contrast(n_neg, goal_count, pooled, head, positives):
    steps, _, width = pooled.shape
    embed = head.shape[1]
    prem_count = steps * SEQS - goal_count
    vmem = pl.BlockSpec(memory_space=pltpu.VMEM)
    return pl.pallas_call(
        functools.partial(contrast_kernel, n_neg, goal_count),
        out_shape=[
            jax.ShapeDtypeStruct((1, goal_count), jnp.float32),
            jax.ShapeDtypeStruct(pooled.shape, jnp.float32),
            jax.ShapeDtypeStruct((2, width // 2, embed), jnp.bfloat16),
        ],
        in_specs=[vmem] * 3,
        out_specs=[vmem] * 3,
        scratch_shapes=[
            pltpu.VMEM((n_neg, 2 * goal_count + prem_count, embed), jnp.bfloat16),
            pltpu.VMEM((n_neg * goal_count, embed), jnp.float32),
            pltpu.VMEM((n_neg * prem_count, embed), jnp.float32),
            pltpu.SemaphoreType.DMA((n_neg,)),
            pltpu.SemaphoreType.DMA((n_neg,)),
        ],
        compiler_params=pltpu.CompilerParams(
            collective_id=0, has_side_effects=True, vmem_limit_bytes=VMEM_LIMIT
        ),
    )(pooled, head, positives)


def upper_kernel(lens_ref, m_ref, d_ref, up_ref, act_ref, scaled_ref, point_ref, sum_ref):
    step = pl.program_id(0)
    count, length, width = m_ref.shape
    tokens = count * length

    @pl.when(step == 0)
    def _():
        sum_ref[...] = jnp.zeros_like(sum_ref)

    rows = up_ref[0] / length_column(lens_ref, step)
    scaled_ref[...] = rows[None]
    mask = length_mask(lens_ref, step, length)
    upstream = jnp.stack([rows[s : s + 1] for s in range(SEQS)]) * mask
    act_grad = (upstream * d_ref[...].astype(jnp.float32)).astype(jnp.bfloat16)
    act_ref[...] = act_grad
    sum_ref[...] += lax.dot_general(
        m_ref[...].reshape(tokens, width),
        act_grad.reshape(tokens, width),
        (((0,), (0,)), ((), ())),
        preferred_element_type=jnp.float32,
    )

    @pl.when(step == pl.num_programs(0) - 1)
    def _():
        for h in range(2):
            point_ref[h] = sum_ref[:, h * width // 2 : (h + 1) * width // 2].astype(jnp.bfloat16)


def run_upper(lens, mixed, slope, pooled_grad):
    total, length, width = mixed.shape
    steps = total // SEQS
    block = pl.BlockSpec((SEQS, length, width), lambda i, lens: (i, 0, 0))
    rows = pl.BlockSpec((1, 8, width), lambda i, lens: (i, 0, 0))
    return pl.pallas_call(
        upper_kernel,
        grid_spec=pltpu.PrefetchScalarGridSpec(
            num_scalar_prefetch=1,
            grid=(steps,),
            in_specs=[block, block, rows],
            out_specs=[
                block,
                rows,
                pl.BlockSpec((2, width, width // 2), lambda i, lens: (0, 0, 0)),
            ],
            scratch_shapes=[pltpu.VMEM((width, width), jnp.float32)],
        ),
        out_shape=[
            jax.ShapeDtypeStruct(mixed.shape, jnp.bfloat16),
            jax.ShapeDtypeStruct(pooled_grad.shape, jnp.float32),
            jax.ShapeDtypeStruct((2, width, width // 2), jnp.bfloat16),
        ],
        compiler_params=pltpu.CompilerParams(vmem_limit_bytes=VMEM_LIMIT),
    )(lens, mixed, slope, pooled_grad)


class Exchange:
    def __init__(self, n_neg, n_rep, mine, pair, slots, full, sems):
        self.mine, self.pair, self.slots, self.full = mine, pair, slots, full
        (self.pair_sems, self.scatter_send, self.scatter_recv,
         self.gather_send, self.gather_recv, self.last_send, self.last_recv) = sems
        self.half_rep = n_rep // 2
        self.chips = n_neg * self.half_rep
        neg, rep = lax.axis_index("neg"), lax.axis_index("rep")
        self.core = lax.rem(rep, 2)
        self.other = 1 - self.core
        self.me = neg * self.half_rep + rep // 2
        self.twin = {"neg": neg, "rep": rep + 1 - 2 * self.core}
        self.share = mine.shape[1] // self.chips

    def device_of(self, chip):
        return {
            "neg": chip // self.half_rep,
            "rep": 2 * lax.rem(chip, self.half_rep) + self.core,
        }

    def peer(self, k):
        return lax.rem(self.me + k, self.chips)

    def rows_of(self, chip):
        return pl.ds(pl.multiple_of(chip * self.share, 16), self.share)

    def copy(self, src, dst, send, recv, device):
        return pltpu.make_async_remote_copy(
            src_ref=src, dst_ref=dst, send_sem=send, recv_sem=recv,
            device_id=device, device_id_type=MESH,
        )

    def pair_copy(self):
        return self.copy(
            self.mine.at[self.other], self.pair, self.pair_sems.at[0], self.pair_sems.at[1],
            self.twin,
        )

    def pair_sum(self):
        self.pair_copy().wait_recv()
        self.mine[self.core] = (
            self.mine[self.core].astype(jnp.float32) + self.pair[...].astype(jnp.float32)
        ).astype(jnp.bfloat16)

    def scatter(self, k):
        chip = self.peer(k)
        return self.copy(
            self.mine.at[self.core, self.rows_of(chip)], self.slots.at[self.me],
            self.scatter_send.at[k], self.scatter_recv.at[self.me], self.device_of(chip),
        )

    def start_scatter(self):
        @pl.loop(1, self.chips)
        def _(k):
            self.scatter(k).start()

        self.slots[self.me] = self.mine[self.core, self.rows_of(self.me)]

    def finish_scatter(self):
        @pl.loop(1, self.chips)
        def _(k):
            chip = self.peer(k)
            self.copy(
                self.slots.at[chip], self.slots.at[chip],
                self.scatter_send.at[k], self.scatter_recv.at[chip], self.device_of(chip),
            ).wait_recv()

        reduced = lax.fori_loop(
            0,
            self.chips,
            lambda c, acc: acc + self.slots[c].astype(jnp.float32),
            jnp.zeros(self.slots.shape[1:], jnp.float32),
        )
        self.full[self.core, self.rows_of(self.me)] = reduced.astype(jnp.bfloat16)

    def gather(self, k, chip):
        block = self.full.at[self.core, self.rows_of(chip)]
        return self.copy(
            block, block, self.gather_send.at[k], self.gather_recv.at[chip],
            self.device_of(self.peer(k)),
        )

    def forward(self, side, chip):
        block = self.full.at[side, self.rows_of(chip)]
        return self.copy(
            block, block, self.last_send.at[chip], self.last_recv.at[chip], self.twin
        )

    def start_gather(self):
        @pl.loop(1, self.chips)
        def _(k):
            self.gather(k, self.me).start()

        self.forward(self.core, self.me).start()

    def finish_gather(self):
        @pl.loop(1, self.chips)
        def _(k):
            chip = self.peer(k)
            self.gather(k, chip).wait_recv()
            self.forward(self.core, chip).start()

    def finish_last(self):
        @pl.loop(0, self.chips)
        def _(chip):
            self.forward(self.other, chip).wait_recv()

    def finish_sends(self):
        self.pair_copy().wait_send()

        @pl.loop(1, self.chips)
        def _(k):
            self.scatter(k).wait_send()
            self.gather(k, self.me).wait_send()

        @pl.loop(0, self.chips)
        def _(chip):
            self.forward(self.core, chip).wait_send()


def lower_kernel(
    n_neg, n_rep, steps,
    n0_ref, m0_ref, d0_ref, n1_ref, a1_ref, inv_ref, up_ref,
    kern_ref, gain_ref, weight_ref, point1_ref, head_ref,
    point_out, head_out, depth_out, gain_out,
    sum_ref, sums_ref,
    mine1, pair1, slots1, full1, mine0, pair0, slots0, full0,
    small_mine, small_pair, small_slots, small_full,
    ps1, ss1, sr1, gs1, gr1, ls1, lr1,
    ps0, ss0, sr0, gs0, gr0, ls0, lr0,
    small_pair_sems, small_send, small_recv, small_last,
):
    step = pl.program_id(0)
    count, length, width = n0_ref.shape
    tokens = count * length
    cols = width // 2
    head_rows = head_ref.shape[1]
    upper = Exchange(n_neg, n_rep, mine1, pair1, slots1, full1, (ps1, ss1, sr1, gs1, gr1, ls1, lr1))
    lower = Exchange(n_neg, n_rep, mine0, pair0, slots0, full0, (ps0, ss0, sr0, gs0, gr0, ls0, lr0))
    chips, core, other, me, twin = lower.chips, lower.core, lower.other, lower.me, lower.twin

    @pl.when(step == 0)
    def _():
        barrier = pltpu.get_barrier_semaphore()
        pl.semaphore_signal(barrier, inc=1, device_id=twin, device_id_type=MESH)

        @pl.loop(1, chips)
        def _(k):
            pl.semaphore_signal(
                barrier, inc=1, device_id=lower.device_of(lower.peer(k)), device_id_type=MESH
            )

        sum_ref[...] = jnp.zeros_like(sum_ref)
        sums_ref[...] = jnp.zeros_like(sums_ref)
        for h in range(2):
            mine1[h, :width] = point1_ref[h]
            mine1[h, width : width + head_rows] = head_ref[h]
            spare = mine1.shape[1] - width - head_rows
            if spare:
                mine1[h, width + head_rows :] = jnp.zeros((spare, cols), jnp.bfloat16)
        pl.semaphore_wait(barrier, chips)
        upper.pair_copy().start()

    @pl.when(step == min(1, steps - 1))
    def _():
        upper.pair_sum()
        upper.start_scatter()

    @pl.when(step == steps // 2)
    def _():
        upper.finish_scatter()
        upper.start_gather()

    def fold(values):
        return jnp.sum(values.reshape(tokens // 8, 8, width), axis=0)

    def conv_terms(act_grad, b, dilation, unscaled):
        conv = lax.dot_general(
            act_grad.reshape(tokens, width),
            weight_ref[b],
            (((1,), (1,)), ((), ())),
            preferred_element_type=jnp.float32,
        ).reshape(count, length, width)
        above = shift_up(conv, dilation)
        below = shift_down(conv, dilation)
        sums_ref[b, 0] += fold(above * unscaled)
        sums_ref[b, 1] += fold(conv * unscaled)
        sums_ref[b, 2] += fold(below * unscaled)
        return above, conv, below

    unscaled = n1_ref[...].astype(jnp.float32)
    above, conv, below = conv_terms(a1_ref[...], 1, UPPER_DILATION, unscaled)
    taps = kern_ref[1] * gain_ref[1][None, :]
    scaled = taps[0] * above + taps[1] * conv + taps[2] * below
    mean = jnp.mean(scaled * unscaled, axis=-1, keepdims=True)
    inverse = inv_ref[:, :, :1]
    rows = up_ref[0]
    upstream = jnp.stack([rows[s : s + 1] for s in range(SEQS)])
    incoming = jnp.where(inverse > 0.0, upstream, 0.0) + inverse * (scaled - unscaled * mean)
    act_grad = (incoming * d0_ref[...].astype(jnp.float32)).astype(jnp.bfloat16)
    sum_ref[...] += lax.dot_general(
        m0_ref[...].reshape(tokens, width),
        act_grad.reshape(tokens, width),
        (((0,), (0,)), ((), ())),
        preferred_element_type=jnp.float32,
    )
    conv_terms(act_grad, 0, LOWER_DILATION, n0_ref[...].astype(jnp.float32))

    @pl.when(step == steps - 1)
    def _():
        spare = mine0.shape[1] - width
        for h in range(2):
            mine0[h, :width] = sum_ref[:, h * cols : (h + 1) * cols].astype(jnp.bfloat16)
            if spare:
                mine0[h, width:] = jnp.zeros((spare, cols), jnp.bfloat16)
        lower.pair_copy().start()
        rows = []
        for b in range(2):
            plain = jnp.sum(sums_ref[b], axis=1)
            rows.append(plain * gain_ref[b][None, :])
            rows.append(jnp.sum(plain * kern_ref[b], axis=0, keepdims=True))
        small = jnp.concatenate([rows[0], rows[2], rows[1], rows[3]], axis=0)
        for h in range(2):
            small_mine[h] = small[:, h * cols : (h + 1) * cols]
        small_copy = lower.copy(
            small_mine.at[other], small_pair, small_pair_sems.at[0], small_pair_sems.at[1], twin
        )
        small_copy.start()
        lower.pair_sum()
        lower.start_scatter()
        small_copy.wait_recv()
        small_slots[me] = small_mine[core] + small_pair[...]

        def small_send_to(k):
            return lower.copy(
                small_slots.at[me], small_slots.at[me], small_send.at[k], small_recv.at[me],
                lower.device_of(lower.peer(k)),
            )

        @pl.loop(1, chips)
        def _(k):
            small_send_to(k).start()

        upper.finish_gather()
        lower.finish_scatter()
        lower.start_gather()

        @pl.loop(1, chips)
        def _(k):
            chip = lower.peer(k)
            lower.copy(
                small_slots.at[chip], small_slots.at[chip], small_send.at[k],
                small_recv.at[chip], lower.device_of(chip),
            ).wait_recv()

        small_full[core] = lax.fori_loop(
            0, chips, lambda c, acc: acc + small_slots[c], jnp.zeros((8, cols), jnp.float32)
        )

        def small_forward(side):
            return lower.copy(
                small_full.at[side], small_full.at[side], small_last.at[0], small_last.at[1], twin
            )

        small_forward(core).start()
        upper.finish_last()
        for h in range(2):
            side = slice(h * cols, (h + 1) * cols)
            point_out[1, :, side] = full1[h, :width]
            head_out[h] = full1[h, width : width + head_rows]
        lower.finish_gather()
        small_forward(other).wait_recv()
        for h in range(2):
            side = slice(h * cols, (h + 1) * cols)
            depth_out[0, :, side] = small_full[h, 0:3]
            depth_out[1, :, side] = small_full[h, 3:6]
            gain_out[:, side] = small_full[h, 6:8]
        lower.finish_last()
        for h in range(2):
            point_out[0, :, h * cols : (h + 1) * cols] = full0[h, :width]
        upper.finish_sends()
        lower.finish_sends()
        small_copy.wait_send()
        small_forward(core).wait_send()

        @pl.loop(1, chips)
        def _(k):
            small_send_to(k).wait_send()


def run_lower(n_neg, n_rep, saved, pooled_grad, kernels, gains, weights, point1, head):
    total, length, width = saved[0].shape
    steps = total // SEQS
    chips = n_neg * n_rep // 2
    cols = width // 2
    grain = 16 * chips
    rows1 = -(-(width + head.shape[1]) // grain) * grain
    rows0 = -(-width // grain) * grain
    block = pl.BlockSpec((SEQS, length, width), lambda i: (i, 0, 0))
    whole = lambda shape: pl.BlockSpec(shape, lambda i: (0,) * len(shape))
    dma = pltpu.SemaphoreType.DMA

    def buffers(rows):
        return [
            pltpu.VMEM((2, rows, cols), jnp.bfloat16),
            pltpu.VMEM((rows, cols), jnp.bfloat16),
            pltpu.VMEM((chips, rows // chips, cols), jnp.bfloat16),
            pltpu.VMEM((2, rows, cols), jnp.bfloat16),
        ]

    outs = [
        jax.ShapeDtypeStruct(weights.shape, jnp.bfloat16),
        jax.ShapeDtypeStruct(head.shape, jnp.bfloat16),
        jax.ShapeDtypeStruct(kernels.shape, jnp.float32),
        jax.ShapeDtypeStruct(gains.shape, jnp.float32),
    ]
    return pl.pallas_call(
        functools.partial(lower_kernel, n_neg, n_rep, steps),
        grid=(steps,),
        in_specs=[block] * 5
        + [
            pl.BlockSpec((SEQS, length, 128), lambda i: (i, 0, 0)),
            pl.BlockSpec((1, 8, width), lambda i: (i, 0, 0)),
            whole(kernels.shape),
            whole(gains.shape),
            whole(weights.shape),
            whole(point1.shape),
            whole(head.shape),
        ],
        out_specs=[whole(out.shape) for out in outs],
        out_shape=outs,
        scratch_shapes=[
            pltpu.VMEM((width, width), jnp.float32),
            pltpu.VMEM((2, 3, 8, width), jnp.float32),
            *buffers(rows1),
            *buffers(rows0),
            pltpu.VMEM((2, 8, cols), jnp.float32),
            pltpu.VMEM((8, cols), jnp.float32),
            pltpu.VMEM((chips, 8, cols), jnp.float32),
            pltpu.VMEM((2, 8, cols), jnp.float32),
            *([dma((2,))] + [dma((chips,))] * 6),
            *([dma((2,))] + [dma((chips,))] * 6),
            dma((2,)),
            dma((chips,)),
            dma((chips,)),
            dma((2,)),
        ],
        compiler_params=pltpu.CompilerParams(
            collective_id=1, has_side_effects=True, vmem_limit_bytes=VMEM_LIMIT
        ),
    )(*saved, pooled_grad, kernels, gains, weights, point1, head)


def local(
    n_neg,
    n_rep,
    goal_states,
    premise_states,
    goal_ids,
    premise_ids,
    positives,
    kernels,
    gains,
    weights,
    head_weight,
):
    goals, premises = goal_states[0], premise_states[0]
    goal_count, length, width = goals.shape
    total = goal_count + premises.shape[0]
    ids = jnp.concatenate([goal_ids[0], premise_ids[0]], axis=0)
    lens = jnp.sum((ids != 0).astype(jnp.int32), axis=1)
    n0, m0, d0, n1, m1, d1, inverse, pooled = run_forward(
        lens, goals, premises, kernels, gains, weights
    )
    loss, pooled_grad, head = run_contrast(n_neg, goal_count, pooled, head_weight, positives)
    act1, upstream, point1 = run_upper(lens, m1, d1, pooled_grad)
    point, head, depth, gain = run_lower(
        n_neg, n_rep, (n0, m0, d0, n1, act1, inverse), upstream, kernels, gains, weights,
        point1, head,
    )
    return (
        loss,
        depth,
        gain,
        point.astype(jnp.float32),
        head.reshape(head_weight.shape).astype(jnp.float32),
    )


def solution(mesh):
    placed = (
        P("rep", "neg", None, None),
        P("rep", "neg", None, None),
        P("rep", "neg", None),
        P("rep", "neg", None),
        P("rep", None),
        P(),
        P(),
        P(),
        P(),
    )
    return jax.shard_map(
        functools.partial(local, mesh.shape["neg"], mesh.shape["rep"]),
        mesh=mesh,
        in_specs=placed,
        out_specs=(P("rep", "neg"), P(), P(), P(), P()),
        check_vma=False,
    )
```

```python
import functools

import jax
import jax.numpy as jnp
from jax import lax
from jax.experimental import pallas as pl
from jax.experimental.pallas import tpu as pltpu
from jax.sharding import PartitionSpec as P

LOWER_DILATION = 4
UPPER_DILATION = 8
LOGIT_SCALE = 20.0
GELU_C = 0.7978845608028654
GELU_A = 0.044715
SEQS = 4
MESH = pl.DeviceIdType.MESH
VMEM_LIMIT = 56 * 1024 * 1024


def shift_down(values, dilation):
    zeros = jnp.zeros_like(values[:, :dilation])
    return jnp.concatenate([zeros, values[:, : values.shape[1] - dilation]], axis=1)


def shift_up(values, dilation):
    zeros = jnp.zeros_like(values[:, :dilation])
    return jnp.concatenate([values[:, dilation:], zeros], axis=1)


def gelu_and_slope(value):
    square = value * value
    bend = jnp.tanh(value * (GELU_C + (GELU_C * GELU_A) * square))
    half = 0.5 + 0.5 * bend
    rest = 0.5 - 0.5 * bend
    slope = half + (half * rest) * (value * (2.0 * GELU_C + (6.0 * GELU_C * GELU_A) * square))
    return value * half, slope


def length_mask(lens_ref, step, length):
    place = lax.broadcasted_iota(jnp.int32, (length, 1), 0)
    return jnp.stack(
        [(place < lens_ref[step * SEQS + s]).astype(jnp.float32) for s in range(SEQS)]
    )


def length_column(lens_ref, step):
    row = lax.broadcasted_iota(jnp.int32, (8, 1), 0)
    spans = jnp.ones((8, 1), jnp.float32)
    for s in range(SEQS):
        spans = jnp.where(row == s, lens_ref[step * SEQS + s].astype(jnp.float32), spans)
    return spans


def forward_kernel(
    goal_steps, lens_ref, goal_ref, prem_ref, kern_ref, gain_ref, weight_ref,
    n0_ref, m0_ref, d0_ref, n1_ref, m1_ref, d1_ref, inv_ref, pool_ref,
):
    step = pl.program_id(0)
    count, length, width = prem_ref.shape
    states = jnp.where(step < goal_steps, goal_ref[...], prem_ref[...])
    mask = length_mask(lens_ref, step, length)

    def block(narrow, b, dilation, n_ref, m_ref, d_ref):
        hidden = narrow.astype(jnp.float32)
        inverse = lax.rsqrt(jnp.mean(hidden * hidden, axis=-1, keepdims=True) + 1e-06) * mask
        unscaled = hidden * inverse
        n_ref[...] = unscaled.astype(jnp.bfloat16)
        taps = kern_ref[b] * gain_ref[b][None, :]
        mixed = (
            taps[0] * shift_down(unscaled, dilation)
            + taps[1] * unscaled
            + taps[2] * shift_up(unscaled, dilation)
        ).astype(jnp.bfloat16)
        m_ref[...] = mixed
        pre_act = jnp.dot(
            mixed.reshape(count * length, width), weight_ref[b], preferred_element_type=jnp.float32
        ).reshape(count, length, width)
        act, slope = gelu_and_slope(pre_act.astype(jnp.bfloat16))
        d_ref[...] = slope
        return narrow + act, inverse

    first, _ = block(states, 0, LOWER_DILATION, n0_ref, m0_ref, d0_ref)
    second, inverse = block(first, 1, UPPER_DILATION, n1_ref, m1_ref, d1_ref)
    inv_ref[...] = jnp.broadcast_to(inverse, inv_ref.shape)
    row = lax.broadcasted_iota(jnp.int32, (8, count * length), 0)
    col = lax.broadcasted_iota(jnp.int32, (8, count * length), 1)
    picks = jnp.zeros((8, count * length), jnp.float32)
    for s in range(SEQS):
        own = (row == s) & (col >= s * length) & (col < s * length + lens_ref[step * SEQS + s])
        picks = jnp.where(own, 1.0, picks)
    sums = jnp.dot(
        picks.astype(jnp.bfloat16),
        second.reshape(count * length, width),
        preferred_element_type=jnp.float32,
    )
    pool_ref[...] = (sums / length_column(lens_ref, step))[None]


def run_forward(lens, goals, premises, kernels, gains, weights):
    goal_count, length, width = goals.shape
    goal_steps = goal_count // SEQS
    total = goal_count + premises.shape[0]
    steps = total // SEQS
    block = pl.BlockSpec((SEQS, length, width), lambda i, lens: (i, 0, 0))
    whole = lambda shape: pl.BlockSpec(shape, lambda i, lens: (0,) * len(shape))
    state = jax.ShapeDtypeStruct((total, length, width), jnp.bfloat16)
    return pl.pallas_call(
        functools.partial(forward_kernel, goal_steps),
        grid_spec=pltpu.PrefetchScalarGridSpec(
            num_scalar_prefetch=1,
            grid=(steps,),
            in_specs=[
                pl.BlockSpec(
                    (SEQS, length, width), lambda i, lens: (jnp.minimum(i, goal_steps - 1), 0, 0)
                ),
                pl.BlockSpec(
                    (SEQS, length, width), lambda i, lens: (jnp.maximum(i - goal_steps, 0), 0, 0)
                ),
                whole(kernels.shape),
                whole(gains.shape),
                whole(weights.shape),
            ],
            out_specs=[block] * 6
            + [
                pl.BlockSpec((SEQS, length, 128), lambda i, lens: (i, 0, 0)),
                pl.BlockSpec((1, 8, width), lambda i, lens: (i, 0, 0)),
            ],
        ),
        out_shape=[state] * 6
        + [
            jax.ShapeDtypeStruct((total, length, 128), jnp.float32),
            jax.ShapeDtypeStruct((steps, 8, width), jnp.float32),
        ],
        compiler_params=pltpu.CompilerParams(vmem_limit_bytes=VMEM_LIMIT),
    )(lens, goals, premises, kernels, gains, weights)


def contrast_kernel(
    n_neg, goal_count, pooled_ref, head_ref, positive_ref,
    loss_ref, pooled_grad_ref, head_grad_ref,
    units_ref, goal_all, prem_all, send_sem, recv_sem,
):
    me = lax.axis_index("neg")
    barrier = pltpu.get_barrier_semaphore()

    @pl.loop(1, n_neg)
    def _(k):
        pl.semaphore_signal(
            barrier, inc=1, device_id={"neg": lax.rem(me + k, n_neg)}, device_id_type=MESH
        )

    steps, _, width = pooled_ref.shape
    goal_steps = goal_count // SEQS
    prem_count = steps * SEQS - goal_count
    pieces = [pooled_ref[i, :SEQS] for i in range(steps)]
    gap = jnp.zeros((goal_count, width), jnp.float32)
    pooled = jnp.concatenate(pieces[:goal_steps] + [gap] + pieces[goal_steps:], axis=0).astype(
        jnp.bfloat16
    )
    head = head_ref[...]
    embedded = jnp.dot(pooled, head, preferred_element_type=jnp.float32)
    magnitude = jnp.sqrt(jnp.sum(embedded * embedded, axis=-1, keepdims=True) + 1e-06)
    unit = embedded / magnitude
    units_ref[me] = unit.astype(jnp.bfloat16)
    pl.semaphore_wait(barrier, n_neg - 1)

    def copy_to(k):
        peer = lax.rem(me + k, n_neg)
        return pltpu.make_async_remote_copy(
            src_ref=units_ref.at[me],
            dst_ref=units_ref.at[me],
            send_sem=send_sem.at[k],
            recv_sem=recv_sem.at[me],
            device_id={"neg": peer},
            device_id_type=MESH,
        )

    @pl.loop(1, n_neg)
    def _(k):
        copy_to(k).start()

    @pl.loop(1, n_neg)
    def _(k):
        source = lax.rem(me + k, n_neg)
        pltpu.make_async_remote_copy(
            src_ref=units_ref.at[source],
            dst_ref=units_ref.at[source],
            send_sem=send_sem.at[k],
            recv_sem=recv_sem.at[source],
            device_id={"neg": source},
            device_id_type=MESH,
        ).wait_recv()

    everyone = units_ref[...].astype(jnp.float32)
    embed = everyone.shape[-1]
    goals = everyone[:, :goal_count].reshape(n_neg * goal_count, embed).astype(jnp.bfloat16)
    premises = everyone[:, 2 * goal_count :].reshape(n_neg * prem_count, embed).astype(jnp.bfloat16)
    scores = LOGIT_SCALE * lax.dot_general(
        premises, goals, (((1,), (1,)), ((), ())), preferred_element_type=jnp.float32
    )
    expon = jnp.exp(scores)
    total = jnp.sum(expon, axis=0, keepdims=True)
    places = lax.broadcasted_iota(jnp.int32, scores.shape, 0)
    onehot = (places == positive_ref[...]).astype(jnp.float32)
    loss = jnp.log(total) - jnp.sum(scores * onehot, axis=0, keepdims=True)
    group = (n_neg * goal_count, goal_count)
    pick = (
        lax.broadcasted_iota(jnp.int32, group, 0)
        == me * goal_count + lax.broadcasted_iota(jnp.int32, group, 1)
    ).astype(jnp.float32)
    loss_ref[...] = jnp.dot(
        jnp.broadcast_to(loss, (8, loss.shape[1])),
        pick,
        precision=lax.Precision.HIGHEST,
        preferred_element_type=jnp.float32,
    )[:1]
    score_grad = ((expon / total - onehot) / goal_count).astype(jnp.bfloat16)
    goal_all[...] = LOGIT_SCALE * lax.dot_general(
        score_grad, premises, (((0,), (0,)), ((), ())), preferred_element_type=jnp.float32
    )
    prem_all[...] = LOGIT_SCALE * jnp.dot(score_grad, goals, preferred_element_type=jnp.float32)
    own_goals = pl.ds(pl.multiple_of(me * goal_count, goal_count), goal_count)
    own_prems = pl.ds(pl.multiple_of(me * prem_count, prem_count), prem_count)
    own_goal_grad = goal_all[own_goals, :]
    unit_grad = jnp.concatenate(
        [own_goal_grad, jnp.zeros_like(own_goal_grad), prem_all[own_prems, :]], axis=0
    )
    embed_grad = (
        (unit_grad - unit * jnp.sum(unit * unit_grad, axis=-1, keepdims=True)) / magnitude
    ).astype(jnp.bfloat16)
    head_grad = lax.dot_general(
        pooled, embed_grad, (((0,), (0,)), ((), ())), preferred_element_type=jnp.float32
    )
    head_grad_ref[...] = head_grad.astype(jnp.bfloat16).reshape(head_grad_ref.shape)
    pooled_grad = lax.dot_general(
        embed_grad, head, (((1,), (1,)), ((), ())), preferred_element_type=jnp.float32
    )
    for i in range(steps):
        start = i * SEQS + (goal_count if i >= goal_steps else 0)
        pooled_grad_ref[i, :SEQS] = pooled_grad[start : start + SEQS]
        pooled_grad_ref[i, SEQS:] = jnp.zeros((8 - SEQS, width), jnp.float32)

    @pl.loop(1, n_neg)
    def _(k):
        copy_to(k).wait_send()


def run_contrast(n_neg, goal_count, pooled, head, positives):
    steps, _, width = pooled.shape
    embed = head.shape[1]
    prem_count = steps * SEQS - goal_count
    vmem = pl.BlockSpec(memory_space=pltpu.VMEM)
    return pl.pallas_call(
        functools.partial(contrast_kernel, n_neg, goal_count),
        out_shape=[
            jax.ShapeDtypeStruct((1, goal_count), jnp.float32),
            jax.ShapeDtypeStruct(pooled.shape, jnp.float32),
            jax.ShapeDtypeStruct((2, width // 2, embed), jnp.bfloat16),
        ],
        in_specs=[vmem] * 3,
        out_specs=[vmem] * 3,
        scratch_shapes=[
            pltpu.VMEM((n_neg, 2 * goal_count + prem_count, embed), jnp.bfloat16),
            pltpu.VMEM((n_neg * goal_count, embed), jnp.float32),
            pltpu.VMEM((n_neg * prem_count, embed), jnp.float32),
            pltpu.SemaphoreType.DMA((n_neg,)),
            pltpu.SemaphoreType.DMA((n_neg,)),
        ],
        compiler_params=pltpu.CompilerParams(
            collective_id=0, has_side_effects=True, vmem_limit_bytes=VMEM_LIMIT
        ),
    )(pooled, head, positives)


def upper_kernel(lens_ref, m_ref, d_ref, up_ref, act_ref, scaled_ref, point_ref, sum_ref):
    step = pl.program_id(0)
    count, length, width = m_ref.shape
    tokens = count * length

    @pl.when(step == 0)
    def _():
        sum_ref[...] = jnp.zeros_like(sum_ref)

    rows = up_ref[0] / length_column(lens_ref, step)
    scaled_ref[...] = rows[None]
    mask = length_mask(lens_ref, step, length)
    upstream = (jnp.stack([rows[s : s + 1] for s in range(SEQS)]) * mask).astype(jnp.bfloat16)
    act_grad = upstream * d_ref[...]
    act_ref[...] = act_grad
    sum_ref[...] += lax.dot_general(
        m_ref[...].reshape(tokens, width),
        act_grad.reshape(tokens, width),
        (((0,), (0,)), ((), ())),
        preferred_element_type=jnp.float32,
    )

    @pl.when(step == pl.num_programs(0) - 1)
    def _():
        for h in range(2):
            point_ref[h] = sum_ref[:, h * width // 2 : (h + 1) * width // 2].astype(jnp.bfloat16)


def run_upper(lens, mixed, slope, pooled_grad):
    total, length, width = mixed.shape
    steps = total // SEQS
    block = pl.BlockSpec((SEQS, length, width), lambda i, lens: (i, 0, 0))
    rows = pl.BlockSpec((1, 8, width), lambda i, lens: (i, 0, 0))
    return pl.pallas_call(
        upper_kernel,
        grid_spec=pltpu.PrefetchScalarGridSpec(
            num_scalar_prefetch=1,
            grid=(steps,),
            in_specs=[block, block, rows],
            out_specs=[
                block,
                rows,
                pl.BlockSpec((2, width, width // 2), lambda i, lens: (0, 0, 0)),
            ],
            scratch_shapes=[pltpu.VMEM((width, width), jnp.float32)],
        ),
        out_shape=[
            jax.ShapeDtypeStruct(mixed.shape, jnp.bfloat16),
            jax.ShapeDtypeStruct(pooled_grad.shape, jnp.float32),
            jax.ShapeDtypeStruct((2, width, width // 2), jnp.bfloat16),
        ],
        compiler_params=pltpu.CompilerParams(vmem_limit_bytes=VMEM_LIMIT),
    )(lens, mixed, slope, pooled_grad)


class Exchange:
    def __init__(self, n_neg, n_rep, mine, pair, slots, full, sems):
        self.mine, self.pair, self.slots, self.full = mine, pair, slots, full
        (self.pair_sems, self.scatter_send, self.scatter_recv,
         self.gather_send, self.gather_recv, self.last_send, self.last_recv) = sems
        self.half_rep = n_rep // 2
        self.chips = n_neg * self.half_rep
        neg, rep = lax.axis_index("neg"), lax.axis_index("rep")
        self.core = lax.rem(rep, 2)
        self.other = 1 - self.core
        self.me = neg * self.half_rep + rep // 2
        self.twin = {"neg": neg, "rep": rep + 1 - 2 * self.core}
        self.share = mine.shape[1] // self.chips

    def device_of(self, chip):
        return {
            "neg": chip // self.half_rep,
            "rep": 2 * lax.rem(chip, self.half_rep) + self.core,
        }

    def peer(self, k):
        return lax.rem(self.me + k, self.chips)

    def rows_of(self, chip):
        return pl.ds(pl.multiple_of(chip * self.share, 16), self.share)

    def copy(self, src, dst, send, recv, device):
        return pltpu.make_async_remote_copy(
            src_ref=src, dst_ref=dst, send_sem=send, recv_sem=recv,
            device_id=device, device_id_type=MESH,
        )

    def pair_copy(self):
        return self.copy(
            self.mine.at[self.other], self.pair, self.pair_sems.at[0], self.pair_sems.at[1],
            self.twin,
        )

    def pair_sum(self):
        self.pair_copy().wait_recv()
        self.mine[self.core] = (
            self.mine[self.core].astype(jnp.float32) + self.pair[...].astype(jnp.float32)
        ).astype(jnp.bfloat16)

    def scatter(self, k):
        chip = self.peer(k)
        return self.copy(
            self.mine.at[self.core, self.rows_of(chip)], self.slots.at[self.me],
            self.scatter_send.at[k], self.scatter_recv.at[self.me], self.device_of(chip),
        )

    def start_scatter(self):
        @pl.loop(1, self.chips)
        def _(k):
            self.scatter(k).start()

        self.slots[self.me] = self.mine[self.core, self.rows_of(self.me)]

    def finish_scatter(self):
        @pl.loop(1, self.chips)
        def _(k):
            chip = self.peer(k)
            self.copy(
                self.slots.at[chip], self.slots.at[chip],
                self.scatter_send.at[k], self.scatter_recv.at[chip], self.device_of(chip),
            ).wait_recv()

        reduced = lax.fori_loop(
            0,
            self.chips,
            lambda c, acc: acc + self.slots[c].astype(jnp.float32),
            jnp.zeros(self.slots.shape[1:], jnp.float32),
        )
        self.full[self.core, self.rows_of(self.me)] = reduced.astype(jnp.bfloat16)

    def gather(self, k, chip):
        block = self.full.at[self.core, self.rows_of(chip)]
        return self.copy(
            block, block, self.gather_send.at[k], self.gather_recv.at[chip],
            self.device_of(self.peer(k)),
        )

    def forward(self, side, chip):
        block = self.full.at[side, self.rows_of(chip)]
        return self.copy(
            block, block, self.last_send.at[chip], self.last_recv.at[chip], self.twin
        )

    def start_gather(self):
        @pl.loop(1, self.chips)
        def _(k):
            self.gather(k, self.me).start()

        self.forward(self.core, self.me).start()

    def finish_gather(self):
        @pl.loop(1, self.chips)
        def _(k):
            chip = self.peer(k)
            self.gather(k, chip).wait_recv()
            self.forward(self.core, chip).start()

    def finish_last(self):
        @pl.loop(0, self.chips)
        def _(chip):
            self.forward(self.other, chip).wait_recv()

    def finish_sends(self):
        self.pair_copy().wait_send()

        @pl.loop(1, self.chips)
        def _(k):
            self.scatter(k).wait_send()
            self.gather(k, self.me).wait_send()

        @pl.loop(0, self.chips)
        def _(chip):
            self.forward(self.core, chip).wait_send()


def lower_kernel(
    n_neg, n_rep, steps,
    n0_ref, m0_ref, d0_ref, n1_ref, a1_ref, inv_ref, up_ref,
    kern_ref, gain_ref, weight_ref, point1_ref, head_ref,
    point_out, head_out, depth_out, gain_out,
    sum_ref, sums_ref,
    mine1, pair1, slots1, full1, mine0, pair0, slots0, full0,
    small_mine, small_pair, small_slots, small_full,
    ps1, ss1, sr1, gs1, gr1, ls1, lr1,
    ps0, ss0, sr0, gs0, gr0, ls0, lr0,
    small_pair_sems, small_send, small_recv, small_last,
):
    step = pl.program_id(0)
    count, length, width = n0_ref.shape
    tokens = count * length
    cols = width // 2
    head_rows = head_ref.shape[1]
    upper = Exchange(n_neg, n_rep, mine1, pair1, slots1, full1, (ps1, ss1, sr1, gs1, gr1, ls1, lr1))
    lower = Exchange(n_neg, n_rep, mine0, pair0, slots0, full0, (ps0, ss0, sr0, gs0, gr0, ls0, lr0))
    chips, core, other, me, twin = lower.chips, lower.core, lower.other, lower.me, lower.twin

    @pl.when(step == 0)
    def _():
        barrier = pltpu.get_barrier_semaphore()
        pl.semaphore_signal(barrier, inc=1, device_id=twin, device_id_type=MESH)

        @pl.loop(1, chips)
        def _(k):
            pl.semaphore_signal(
                barrier, inc=1, device_id=lower.device_of(lower.peer(k)), device_id_type=MESH
            )

        sum_ref[...] = jnp.zeros_like(sum_ref)
        sums_ref[...] = jnp.zeros_like(sums_ref)
        for h in range(2):
            mine1[h, :width] = point1_ref[h]
            mine1[h, width : width + head_rows] = head_ref[h]
            spare = mine1.shape[1] - width - head_rows
            if spare:
                mine1[h, width + head_rows :] = jnp.zeros((spare, cols), jnp.bfloat16)

    @pl.when(step == 1)
    def _():
        pl.semaphore_wait(pltpu.get_barrier_semaphore(), chips)
        upper.pair_copy().start()

    @pl.when(step == 2)
    def _():
        upper.pair_sum()
        upper.start_scatter()

    @pl.when(step == (2 * steps) // 3)
    def _():
        upper.finish_scatter()
        upper.start_gather()

    def fold(values):
        return jnp.sum(values.reshape(tokens // 8, 8, width), axis=0)

    def conv_terms(act_grad, b, dilation, unscaled):
        conv = lax.dot_general(
            act_grad.reshape(tokens, width),
            weight_ref[b],
            (((1,), (1,)), ((), ())),
            preferred_element_type=jnp.float32,
        ).reshape(count, length, width)
        above = shift_up(conv, dilation)
        below = shift_down(conv, dilation)
        sums_ref[b, 0] += fold(above * unscaled)
        sums_ref[b, 1] += fold(conv * unscaled)
        sums_ref[b, 2] += fold(below * unscaled)
        return above, conv, below

    unscaled = n1_ref[...].astype(jnp.float32)
    above, conv, below = conv_terms(a1_ref[...], 1, UPPER_DILATION, unscaled)
    taps = kern_ref[1] * gain_ref[1][None, :]
    scaled = taps[0] * above + taps[1] * conv + taps[2] * below
    mean = jnp.mean(scaled * unscaled, axis=-1, keepdims=True)
    inverse = inv_ref[:, :, :1]
    rows = up_ref[0]
    upstream = jnp.stack([rows[s : s + 1] for s in range(SEQS)])
    incoming = jnp.where(inverse > 0.0, upstream, 0.0) + inverse * (scaled - unscaled * mean)
    act_grad = incoming.astype(jnp.bfloat16) * d0_ref[...]
    sum_ref[...] += lax.dot_general(
        m0_ref[...].reshape(tokens, width),
        act_grad.reshape(tokens, width),
        (((0,), (0,)), ((), ())),
        preferred_element_type=jnp.float32,
    )
    conv_terms(act_grad, 0, LOWER_DILATION, n0_ref[...].astype(jnp.float32))

    @pl.when(step == steps - 1)
    def _():
        spare = mine0.shape[1] - width
        for h in range(2):
            mine0[h, :width] = sum_ref[:, h * cols : (h + 1) * cols].astype(jnp.bfloat16)
            if spare:
                mine0[h, width:] = jnp.zeros((spare, cols), jnp.bfloat16)
        lower.pair_copy().start()
        rows = []
        for b in range(2):
            plain = jnp.sum(sums_ref[b], axis=1)
            rows.append(plain * gain_ref[b][None, :])
            rows.append(jnp.sum(plain * kern_ref[b], axis=0, keepdims=True))
        small = jnp.concatenate([rows[0], rows[2], rows[1], rows[3]], axis=0)
        for h in range(2):
            small_mine[h] = small[:, h * cols : (h + 1) * cols]
        small_copy = lower.copy(
            small_mine.at[other], small_pair, small_pair_sems.at[0], small_pair_sems.at[1], twin
        )
        small_copy.start()
        lower.pair_sum()
        lower.start_scatter()
        small_copy.wait_recv()
        small_slots[me] = small_mine[core] + small_pair[...]

        def small_send_to(k):
            return lower.copy(
                small_slots.at[me], small_slots.at[me], small_send.at[k], small_recv.at[me],
                lower.device_of(lower.peer(k)),
            )

        @pl.loop(1, chips)
        def _(k):
            small_send_to(k).start()

        upper.finish_gather()
        lower.finish_scatter()
        lower.start_gather()

        @pl.loop(1, chips)
        def _(k):
            chip = lower.peer(k)
            lower.copy(
                small_slots.at[chip], small_slots.at[chip], small_send.at[k],
                small_recv.at[chip], lower.device_of(chip),
            ).wait_recv()

        small_full[core] = lax.fori_loop(
            0, chips, lambda c, acc: acc + small_slots[c], jnp.zeros((8, cols), jnp.float32)
        )

        def small_forward(side):
            return lower.copy(
                small_full.at[side], small_full.at[side], small_last.at[0], small_last.at[1], twin
            )

        small_forward(core).start()
        upper.finish_last()
        for h in range(2):
            side = slice(h * cols, (h + 1) * cols)
            point_out[1, :, side] = full1[h, :width]
            head_out[h] = full1[h, width : width + head_rows]
        lower.finish_gather()
        small_forward(other).wait_recv()
        for h in range(2):
            side = slice(h * cols, (h + 1) * cols)
            depth_out[0, :, side] = small_full[h, 0:3]
            depth_out[1, :, side] = small_full[h, 3:6]
            gain_out[:, side] = small_full[h, 6:8]
        lower.finish_last()
        for h in range(2):
            point_out[0, :, h * cols : (h + 1) * cols] = full0[h, :width]
        upper.finish_sends()
        lower.finish_sends()
        small_copy.wait_send()
        small_forward(core).wait_send()

        @pl.loop(1, chips)
        def _(k):
            small_send_to(k).wait_send()


def run_lower(n_neg, n_rep, saved, pooled_grad, kernels, gains, weights, point1, head):
    total, length, width = saved[0].shape
    steps = total // SEQS
    assert steps >= 5
    chips = n_neg * n_rep // 2
    cols = width // 2
    grain = 16 * chips
    rows1 = -(-(width + head.shape[1]) // grain) * grain
    rows0 = -(-width // grain) * grain
    block = pl.BlockSpec((SEQS, length, width), lambda i: (i, 0, 0))
    whole = lambda shape: pl.BlockSpec(shape, lambda i: (0,) * len(shape))
    dma = pltpu.SemaphoreType.DMA

    def buffers(rows):
        return [
            pltpu.VMEM((2, rows, cols), jnp.bfloat16),
            pltpu.VMEM((rows, cols), jnp.bfloat16),
            pltpu.VMEM((chips, rows // chips, cols), jnp.bfloat16),
            pltpu.VMEM((2, rows, cols), jnp.bfloat16),
        ]

    outs = [
        jax.ShapeDtypeStruct(weights.shape, jnp.bfloat16),
        jax.ShapeDtypeStruct(head.shape, jnp.bfloat16),
        jax.ShapeDtypeStruct(kernels.shape, jnp.float32),
        jax.ShapeDtypeStruct(gains.shape, jnp.float32),
    ]
    return pl.pallas_call(
        functools.partial(lower_kernel, n_neg, n_rep, steps),
        grid=(steps,),
        in_specs=[block] * 5
        + [
            pl.BlockSpec((SEQS, length, 128), lambda i: (i, 0, 0)),
            pl.BlockSpec((1, 8, width), lambda i: (i, 0, 0)),
            whole(kernels.shape),
            whole(gains.shape),
            whole(weights.shape),
            whole(point1.shape),
            whole(head.shape),
        ],
        out_specs=[whole(out.shape) for out in outs],
        out_shape=outs,
        scratch_shapes=[
            pltpu.VMEM((width, width), jnp.float32),
            pltpu.VMEM((2, 3, 8, width), jnp.float32),
            *buffers(rows1),
            *buffers(rows0),
            pltpu.VMEM((2, 8, cols), jnp.float32),
            pltpu.VMEM((8, cols), jnp.float32),
            pltpu.VMEM((chips, 8, cols), jnp.float32),
            pltpu.VMEM((2, 8, cols), jnp.float32),
            *([dma((2,))] + [dma((chips,))] * 6),
            *([dma((2,))] + [dma((chips,))] * 6),
            dma((2,)),
            dma((chips,)),
            dma((chips,)),
            dma((2,)),
        ],
        compiler_params=pltpu.CompilerParams(
            collective_id=1, has_side_effects=True, vmem_limit_bytes=VMEM_LIMIT
        ),
    )(*saved, pooled_grad, kernels, gains, weights, point1, head)


def widen_kernel(point_ref, head_ref, loss_ref, point_out, head_out, loss_out):
    point_out[...] = point_ref[...].astype(jnp.float32)
    head_out[...] = head_ref[0].astype(jnp.float32)
    loss_out[...] = loss_ref[...]


def run_widen(point, head, loss):
    _, width, embed = head.shape
    part = point.shape[1] // 2
    rows = width // 2
    return pl.pallas_call(
        widen_kernel,
        grid=(4,),
        in_specs=[
            pl.BlockSpec((1, part, point.shape[2]), lambda i: (i // 2, i % 2, 0)),
            pl.BlockSpec((1, rows, embed), lambda i: (i // 2, i % 2, 0)),
            pl.BlockSpec(loss.shape, lambda i: (0, 0)),
        ],
        out_specs=[
            pl.BlockSpec((1, part, point.shape[2]), lambda i: (i // 2, i % 2, 0)),
            pl.BlockSpec((rows, embed), lambda i: (i, 0)),
            pl.BlockSpec(loss.shape, lambda i: (0, 0)),
        ],
        out_shape=[
            jax.ShapeDtypeStruct(point.shape, jnp.float32),
            jax.ShapeDtypeStruct((2 * width, embed), jnp.float32),
            jax.ShapeDtypeStruct(loss.shape, jnp.float32),
        ],
    )(point, head, loss)


def local(
    n_neg,
    n_rep,
    goal_states,
    premise_states,
    goal_ids,
    premise_ids,
    positives,
    kernels,
    gains,
    weights,
    head_weight,
):
    goals, premises = goal_states[0], premise_states[0]
    goal_count, length, width = goals.shape
    total = goal_count + premises.shape[0]
    ids = jnp.concatenate([goal_ids[0], premise_ids[0]], axis=0)
    lens = jnp.sum((ids != 0).astype(jnp.int32), axis=1)
    n0, m0, d0, n1, m1, d1, inverse, pooled = run_forward(
        lens, goals, premises, kernels, gains, weights
    )
    loss, pooled_grad, head = run_contrast(n_neg, goal_count, pooled, head_weight, positives)
    act1, upstream, point1 = run_upper(lens, m1, d1, pooled_grad)
    point, head, depth, gain = run_lower(
        n_neg, n_rep, (n0, m0, d0, n1, act1, inverse), upstream, kernels, gains, weights,
        point1, head,
    )
    point, head, loss = run_widen(point, head, loss)
    return loss, depth, gain, point, head


def solution(mesh):
    placed = (
        P("rep", "neg", None, None),
        P("rep", "neg", None, None),
        P("rep", "neg", None),
        P("rep", "neg", None),
        P("rep", None),
        P(),
        P(),
        P(),
        P(),
    )
    return jax.shard_map(
        functools.partial(local, mesh.shape["neg"], mesh.shape["rep"]),
        mesh=mesh,
        in_specs=placed,
        out_specs=(P("rep", "neg"), P(), P(), P(), P()),
        check_vma=False,
    )
```

```python
import functools

import jax
import jax.numpy as jnp
from jax import lax
from jax.experimental import pallas as pl
from jax.experimental.pallas import tpu as pltpu
from jax.sharding import PartitionSpec as P

LOWER_DILATION = 4
UPPER_DILATION = 8
LOGIT_SCALE = 20.0
GELU_C = 0.7978845608028654
GELU_A = 0.044715
SEQS = 4
GROUPS = 2
MESH = pl.DeviceIdType.MESH
VMEM_LIMIT = 56 * 1024 * 1024


def shift_down(values, dilation):
    zeros = jnp.zeros_like(values[:, :dilation])
    return jnp.concatenate([zeros, values[:, : values.shape[1] - dilation]], axis=1)


def shift_up(values, dilation):
    zeros = jnp.zeros_like(values[:, :dilation])
    return jnp.concatenate([values[:, dilation:], zeros], axis=1)


def gelu_and_slope(value):
    square = value * value
    bend = jnp.tanh(value * (GELU_C + (GELU_C * GELU_A) * square))
    half = 0.5 + 0.5 * bend
    rest = 0.5 - 0.5 * bend
    slope = half + (half * rest) * (value * (2.0 * GELU_C + (6.0 * GELU_C * GELU_A) * square))
    return value * half, slope


def length_mask(lens_ref, step, length):
    place = lax.broadcasted_iota(jnp.int32, (length, 1), 0)
    return jnp.stack(
        [(place < lens_ref[step * SEQS + s]).astype(jnp.float32) for s in range(SEQS)]
    )


def length_column(lens_ref, step):
    row = lax.broadcasted_iota(jnp.int32, (8, 1), 0)
    spans = jnp.ones((8, 1), jnp.float32)
    for s in range(SEQS):
        spans = jnp.where(row == s, lens_ref[step * SEQS + s].astype(jnp.float32), spans)
    return spans


def forward_kernel(
    goal_steps, lens_ref, goal_ref, prem_ref, kern_ref, gain_ref, weight_ref,
    n0_ref, m0_ref, d0_ref, n1_ref, m1_ref, d1_ref, inv_ref, pool_ref,
):
    step = pl.program_id(0)
    count, length, width = prem_ref.shape
    states = jnp.where(step < goal_steps, goal_ref[...], prem_ref[...])
    mask = length_mask(lens_ref, step, length)

    def block(narrow, b, dilation, n_ref, m_ref, d_ref):
        hidden = narrow.astype(jnp.float32)
        inverse = lax.rsqrt(jnp.mean(hidden * hidden, axis=-1, keepdims=True) + 1e-06) * mask
        unscaled = hidden * inverse
        n_ref[...] = unscaled.astype(jnp.bfloat16)
        taps = kern_ref[b] * gain_ref[b][None, :]
        mixed = (
            taps[0] * shift_down(unscaled, dilation)
            + taps[1] * unscaled
            + taps[2] * shift_up(unscaled, dilation)
        ).astype(jnp.bfloat16)
        m_ref[...] = mixed
        pre_act = jnp.dot(
            mixed.reshape(count * length, width), weight_ref[b], preferred_element_type=jnp.float32
        ).reshape(count, length, width)
        act, slope = gelu_and_slope(pre_act.astype(jnp.bfloat16))
        d_ref[...] = slope
        return narrow + act, inverse

    first, _ = block(states, 0, LOWER_DILATION, n0_ref, m0_ref, d0_ref)
    second, inverse = block(first, 1, UPPER_DILATION, n1_ref, m1_ref, d1_ref)
    inv_ref[...] = jnp.broadcast_to(inverse, inv_ref.shape)
    row = lax.broadcasted_iota(jnp.int32, (8, count * length), 0)
    col = lax.broadcasted_iota(jnp.int32, (8, count * length), 1)
    picks = jnp.zeros((8, count * length), jnp.float32)
    for s in range(SEQS):
        own = (row == s) & (col >= s * length) & (col < s * length + lens_ref[step * SEQS + s])
        picks = jnp.where(own, 1.0, picks)
    sums = jnp.dot(
        picks.astype(jnp.bfloat16),
        second.reshape(count * length, width),
        preferred_element_type=jnp.float32,
    )
    pool_ref[...] = (sums / length_column(lens_ref, step))[None]


def run_forward(lens, goals, premises, kernels, gains, weights):
    goal_count, length, width = goals.shape
    goal_steps = goal_count // SEQS
    total = goal_count + premises.shape[0]
    steps = total // SEQS
    block = pl.BlockSpec((SEQS, length, width), lambda i, lens: (i, 0, 0))
    whole = lambda shape: pl.BlockSpec(shape, lambda i, lens: (0,) * len(shape))
    state = jax.ShapeDtypeStruct((total, length, width), jnp.bfloat16)
    return pl.pallas_call(
        functools.partial(forward_kernel, goal_steps),
        grid_spec=pltpu.PrefetchScalarGridSpec(
            num_scalar_prefetch=1,
            grid=(steps,),
            in_specs=[
                pl.BlockSpec(
                    (SEQS, length, width), lambda i, lens: (jnp.minimum(i, goal_steps - 1), 0, 0)
                ),
                pl.BlockSpec(
                    (SEQS, length, width), lambda i, lens: (jnp.maximum(i - goal_steps, 0), 0, 0)
                ),
                whole(kernels.shape),
                whole(gains.shape),
                whole(weights.shape),
            ],
            out_specs=[block] * 6
            + [
                pl.BlockSpec((SEQS, length, 128), lambda i, lens: (i, 0, 0)),
                pl.BlockSpec((1, 8, width), lambda i, lens: (i, 0, 0)),
            ],
        ),
        out_shape=[state] * 6
        + [
            jax.ShapeDtypeStruct((total, length, 128), jnp.float32),
            jax.ShapeDtypeStruct((steps, 8, width), jnp.float32),
        ],
        compiler_params=pltpu.CompilerParams(vmem_limit_bytes=VMEM_LIMIT),
    )(lens, goals, premises, kernels, gains, weights)


def contrast_kernel(
    n_neg, goal_count, pooled_ref, head_ref, positive_ref,
    loss_ref, pooled_grad_ref, head_grad_ref,
    units_ref, goal_all, prem_all, send_sem, recv_sem,
):
    me = lax.axis_index("neg")
    barrier = pltpu.get_barrier_semaphore()

    @pl.loop(1, n_neg)
    def _(k):
        pl.semaphore_signal(
            barrier, inc=1, device_id={"neg": lax.rem(me + k, n_neg)}, device_id_type=MESH
        )

    steps, _, width = pooled_ref.shape
    goal_steps = goal_count // SEQS
    prem_count = steps * SEQS - goal_count
    pieces = [pooled_ref[i, :SEQS] for i in range(steps)]
    gap = jnp.zeros((goal_count, width), jnp.float32)
    pooled = jnp.concatenate(pieces[:goal_steps] + [gap] + pieces[goal_steps:], axis=0).astype(
        jnp.bfloat16
    )
    head = head_ref[...]
    embedded = jnp.dot(pooled, head, preferred_element_type=jnp.float32)
    magnitude = jnp.sqrt(jnp.sum(embedded * embedded, axis=-1, keepdims=True) + 1e-06)
    unit = embedded / magnitude
    units_ref[me] = unit.astype(jnp.bfloat16)
    pl.semaphore_wait(barrier, n_neg - 1)

    def copy_to(k):
        peer = lax.rem(me + k, n_neg)
        return pltpu.make_async_remote_copy(
            src_ref=units_ref.at[me],
            dst_ref=units_ref.at[me],
            send_sem=send_sem.at[k],
            recv_sem=recv_sem.at[me],
            device_id={"neg": peer},
            device_id_type=MESH,
        )

    @pl.loop(1, n_neg)
    def _(k):
        copy_to(k).start()

    @pl.loop(1, n_neg)
    def _(k):
        source = lax.rem(me + k, n_neg)
        pltpu.make_async_remote_copy(
            src_ref=units_ref.at[source],
            dst_ref=units_ref.at[source],
            send_sem=send_sem.at[k],
            recv_sem=recv_sem.at[source],
            device_id={"neg": source},
            device_id_type=MESH,
        ).wait_recv()

    everyone = units_ref[...].astype(jnp.float32)
    embed = everyone.shape[-1]
    goals = everyone[:, :goal_count].reshape(n_neg * goal_count, embed).astype(jnp.bfloat16)
    premises = everyone[:, 2 * goal_count :].reshape(n_neg * prem_count, embed).astype(jnp.bfloat16)
    scores = LOGIT_SCALE * lax.dot_general(
        premises, goals, (((1,), (1,)), ((), ())), preferred_element_type=jnp.float32
    )
    expon = jnp.exp(scores)
    total = jnp.sum(expon, axis=0, keepdims=True)
    places = lax.broadcasted_iota(jnp.int32, scores.shape, 0)
    onehot = (places == positive_ref[...]).astype(jnp.float32)
    loss = jnp.log(total) - jnp.sum(scores * onehot, axis=0, keepdims=True)
    group = (n_neg * goal_count, goal_count)
    pick = (
        lax.broadcasted_iota(jnp.int32, group, 0)
        == me * goal_count + lax.broadcasted_iota(jnp.int32, group, 1)
    ).astype(jnp.float32)
    loss_ref[...] = jnp.dot(
        jnp.broadcast_to(loss, (8, loss.shape[1])),
        pick,
        precision=lax.Precision.HIGHEST,
        preferred_element_type=jnp.float32,
    )[:1]
    score_grad = ((expon / total - onehot) / goal_count).astype(jnp.bfloat16)
    goal_all[...] = LOGIT_SCALE * lax.dot_general(
        score_grad, premises, (((0,), (0,)), ((), ())), preferred_element_type=jnp.float32
    )
    prem_all[...] = LOGIT_SCALE * jnp.dot(score_grad, goals, preferred_element_type=jnp.float32)
    own_goals = pl.ds(pl.multiple_of(me * goal_count, goal_count), goal_count)
    own_prems = pl.ds(pl.multiple_of(me * prem_count, prem_count), prem_count)
    own_goal_grad = goal_all[own_goals, :]
    unit_grad = jnp.concatenate(
        [own_goal_grad, jnp.zeros_like(own_goal_grad), prem_all[own_prems, :]], axis=0
    )
    embed_grad = (
        (unit_grad - unit * jnp.sum(unit * unit_grad, axis=-1, keepdims=True)) / magnitude
    ).astype(jnp.bfloat16)
    head_grad = lax.dot_general(
        pooled, embed_grad, (((0,), (0,)), ((), ())), preferred_element_type=jnp.float32
    )
    head_grad_ref[...] = head_grad.astype(jnp.bfloat16).reshape(head_grad_ref.shape)
    pooled_grad = lax.dot_general(
        embed_grad, head, (((1,), (1,)), ((), ())), preferred_element_type=jnp.float32
    )
    for i in range(steps):
        start = i * SEQS + (goal_count if i >= goal_steps else 0)
        pooled_grad_ref[i, :SEQS] = pooled_grad[start : start + SEQS]
        pooled_grad_ref[i, SEQS:] = jnp.zeros((8 - SEQS, width), jnp.float32)

    @pl.loop(1, n_neg)
    def _(k):
        copy_to(k).wait_send()


def run_contrast(n_neg, goal_count, pooled, head, positives):
    steps, _, width = pooled.shape
    embed = head.shape[1]
    prem_count = steps * SEQS - goal_count
    vmem = pl.BlockSpec(memory_space=pltpu.VMEM)
    return pl.pallas_call(
        functools.partial(contrast_kernel, n_neg, goal_count),
        out_shape=[
            jax.ShapeDtypeStruct((1, goal_count), jnp.float32),
            jax.ShapeDtypeStruct(pooled.shape, jnp.float32),
            jax.ShapeDtypeStruct((2, width // 2, embed), jnp.bfloat16),
        ],
        in_specs=[vmem] * 3,
        out_specs=[vmem] * 3,
        scratch_shapes=[
            pltpu.VMEM((n_neg, 2 * goal_count + prem_count, embed), jnp.bfloat16),
            pltpu.VMEM((n_neg * goal_count, embed), jnp.float32),
            pltpu.VMEM((n_neg * prem_count, embed), jnp.float32),
            pltpu.SemaphoreType.DMA((n_neg,)),
            pltpu.SemaphoreType.DMA((n_neg,)),
        ],
        compiler_params=pltpu.CompilerParams(
            collective_id=0, has_side_effects=True, vmem_limit_bytes=VMEM_LIMIT
        ),
    )(pooled, head, positives)


def upper_kernel(lens_ref, m_ref, d_ref, up_ref, act_ref, scaled_ref, point_ref, sum_ref):
    step = pl.program_id(0)
    count, length, width = m_ref.shape
    tokens = count * length

    @pl.when(step == 0)
    def _():
        sum_ref[...] = jnp.zeros_like(sum_ref)

    rows, mask = [], []
    for j in range(GROUPS):
        part = step * GROUPS + j
        rows.append(up_ref[j] / length_column(lens_ref, part))
        scaled_ref[j] = rows[j]
        mask.append(length_mask(lens_ref, part, length))
    mask = jnp.concatenate(mask, axis=0)
    spread = jnp.stack([row[s : s + 1] for row in rows for s in range(SEQS)])
    upstream = (spread * mask).astype(jnp.bfloat16)
    act_grad = upstream * d_ref[...]
    act_ref[...] = act_grad
    sum_ref[...] += lax.dot_general(
        m_ref[...].reshape(tokens, width),
        act_grad.reshape(tokens, width),
        (((0,), (0,)), ((), ())),
        preferred_element_type=jnp.float32,
    )

    @pl.when(step == pl.num_programs(0) - 1)
    def _():
        for h in range(2):
            point_ref[h] = sum_ref[:, h * width // 2 : (h + 1) * width // 2].astype(jnp.bfloat16)


def run_upper(lens, mixed, slope, pooled_grad):
    total, length, width = mixed.shape
    steps = total // (GROUPS * SEQS)
    assert total % (GROUPS * SEQS) == 0
    block = pl.BlockSpec((GROUPS * SEQS, length, width), lambda i, lens: (i, 0, 0))
    rows = pl.BlockSpec((GROUPS, 8, width), lambda i, lens: (i, 0, 0))
    return pl.pallas_call(
        upper_kernel,
        grid_spec=pltpu.PrefetchScalarGridSpec(
            num_scalar_prefetch=1,
            grid=(steps,),
            in_specs=[block, block, rows],
            out_specs=[
                block,
                rows,
                pl.BlockSpec((2, width, width // 2), lambda i, lens: (0, 0, 0)),
            ],
            scratch_shapes=[pltpu.VMEM((width, width), jnp.float32)],
        ),
        out_shape=[
            jax.ShapeDtypeStruct(mixed.shape, jnp.bfloat16),
            jax.ShapeDtypeStruct(pooled_grad.shape, jnp.float32),
            jax.ShapeDtypeStruct((2, width, width // 2), jnp.bfloat16),
        ],
        compiler_params=pltpu.CompilerParams(vmem_limit_bytes=VMEM_LIMIT),
    )(lens, mixed, slope, pooled_grad)


class Exchange:
    def __init__(self, n_neg, n_rep, mine, pair, slots, full, sems):
        self.mine, self.pair, self.slots, self.full = mine, pair, slots, full
        (self.pair_sems, self.scatter_send, self.scatter_recv,
         self.gather_send, self.gather_recv, self.last_send, self.last_recv) = sems
        self.half_rep = n_rep // 2
        self.chips = n_neg * self.half_rep
        neg, rep = lax.axis_index("neg"), lax.axis_index("rep")
        self.core = lax.rem(rep, 2)
        self.other = 1 - self.core
        self.me = neg * self.half_rep + rep // 2
        self.twin = {"neg": neg, "rep": rep + 1 - 2 * self.core}
        self.share = mine.shape[1] // self.chips

    def device_of(self, chip):
        return {
            "neg": chip // self.half_rep,
            "rep": 2 * lax.rem(chip, self.half_rep) + self.core,
        }

    def peer(self, k):
        return lax.rem(self.me + k, self.chips)

    def rows_of(self, chip):
        return pl.ds(pl.multiple_of(chip * self.share, 16), self.share)

    def copy(self, src, dst, send, recv, device):
        return pltpu.make_async_remote_copy(
            src_ref=src, dst_ref=dst, send_sem=send, recv_sem=recv,
            device_id=device, device_id_type=MESH,
        )

    def pair_copy(self):
        return self.copy(
            self.mine.at[self.other], self.pair, self.pair_sems.at[0], self.pair_sems.at[1],
            self.twin,
        )

    def pair_sum(self):
        self.pair_copy().wait_recv()
        self.mine[self.core] = (
            self.mine[self.core].astype(jnp.float32) + self.pair[...].astype(jnp.float32)
        ).astype(jnp.bfloat16)

    def scatter(self, k):
        chip = self.peer(k)
        return self.copy(
            self.mine.at[self.core, self.rows_of(chip)], self.slots.at[self.me],
            self.scatter_send.at[k], self.scatter_recv.at[self.me], self.device_of(chip),
        )

    def start_scatter(self):
        @pl.loop(1, self.chips)
        def _(k):
            self.scatter(k).start()

        self.slots[self.me] = self.mine[self.core, self.rows_of(self.me)]

    def finish_scatter(self):
        @pl.loop(1, self.chips)
        def _(k):
            chip = self.peer(k)
            self.copy(
                self.slots.at[chip], self.slots.at[chip],
                self.scatter_send.at[k], self.scatter_recv.at[chip], self.device_of(chip),
            ).wait_recv()

        reduced = lax.fori_loop(
            0,
            self.chips,
            lambda c, acc: acc + self.slots[c].astype(jnp.float32),
            jnp.zeros(self.slots.shape[1:], jnp.float32),
        )
        self.full[self.core, self.rows_of(self.me)] = reduced.astype(jnp.bfloat16)

    def gather(self, k, chip):
        block = self.full.at[self.core, self.rows_of(chip)]
        return self.copy(
            block, block, self.gather_send.at[k], self.gather_recv.at[chip],
            self.device_of(self.peer(k)),
        )

    def forward(self, side, chip):
        block = self.full.at[side, self.rows_of(chip)]
        return self.copy(
            block, block, self.last_send.at[chip], self.last_recv.at[chip], self.twin
        )

    def start_gather(self):
        @pl.loop(1, self.chips)
        def _(k):
            self.gather(k, self.me).start()

        self.forward(self.core, self.me).start()

    def finish_gather(self):
        @pl.loop(1, self.chips)
        def _(k):
            chip = self.peer(k)
            self.gather(k, chip).wait_recv()
            self.forward(self.core, chip).start()

    def finish_last(self):
        @pl.loop(0, self.chips)
        def _(chip):
            self.forward(self.other, chip).wait_recv()

    def finish_sends(self):
        self.pair_copy().wait_send()

        @pl.loop(1, self.chips)
        def _(k):
            self.scatter(k).wait_send()
            self.gather(k, self.me).wait_send()

        @pl.loop(0, self.chips)
        def _(chip):
            self.forward(self.core, chip).wait_send()


def lower_kernel(
    n_neg, n_rep, steps,
    n0_ref, m0_ref, d0_ref, n1_ref, a1_ref, inv_ref, up_ref,
    kern_ref, gain_ref, weight_ref, point1_ref, head_ref,
    point_out, head_out, depth_out, gain_out,
    sum_ref, sums_ref,
    mine1, pair1, slots1, full1, mine0, pair0, slots0, full0,
    small_mine, small_pair, small_slots, small_full,
    ps1, ss1, sr1, gs1, gr1, ls1, lr1,
    ps0, ss0, sr0, gs0, gr0, ls0, lr0,
    small_pair_sems, small_send, small_recv, small_last,
):
    step = pl.program_id(0)
    count, length, width = n0_ref.shape
    tokens = count * length
    cols = width // 2
    head_rows = head_ref.shape[1]
    upper = Exchange(n_neg, n_rep, mine1, pair1, slots1, full1, (ps1, ss1, sr1, gs1, gr1, ls1, lr1))
    lower = Exchange(n_neg, n_rep, mine0, pair0, slots0, full0, (ps0, ss0, sr0, gs0, gr0, ls0, lr0))
    chips, core, other, me, twin = lower.chips, lower.core, lower.other, lower.me, lower.twin

    @pl.when(step == 0)
    def _():
        barrier = pltpu.get_barrier_semaphore()
        pl.semaphore_signal(barrier, inc=1, device_id=twin, device_id_type=MESH)

        @pl.loop(1, chips)
        def _(k):
            pl.semaphore_signal(
                barrier, inc=1, device_id=lower.device_of(lower.peer(k)), device_id_type=MESH
            )

        sum_ref[...] = jnp.zeros_like(sum_ref)
        sums_ref[...] = jnp.zeros_like(sums_ref)
        for h in range(2):
            mine1[h, :width] = point1_ref[h]
            mine1[h, width : width + head_rows] = head_ref[h]
            spare = mine1.shape[1] - width - head_rows
            if spare:
                mine1[h, width + head_rows :] = jnp.zeros((spare, cols), jnp.bfloat16)

    @pl.when(step == 1)
    def _():
        pl.semaphore_wait(pltpu.get_barrier_semaphore(), chips)
        upper.pair_copy().start()

    @pl.when(step == 2)
    def _():
        upper.pair_sum()
        upper.start_scatter()

    @pl.when(step == (2 * steps) // 3)
    def _():
        upper.finish_scatter()
        upper.start_gather()

    def fold(values):
        return jnp.sum(values.reshape(tokens // 8, 8, width), axis=0)

    def conv_terms(act_grad, b, dilation, unscaled):
        conv = lax.dot_general(
            act_grad.reshape(tokens, width),
            weight_ref[b],
            (((1,), (1,)), ((), ())),
            preferred_element_type=jnp.float32,
        ).reshape(count, length, width)
        above = shift_up(conv, dilation)
        below = shift_down(conv, dilation)
        sums_ref[b, 0] += fold(above * unscaled)
        sums_ref[b, 1] += fold(conv * unscaled)
        sums_ref[b, 2] += fold(below * unscaled)
        return above, conv, below

    unscaled = n1_ref[...].astype(jnp.float32)
    above, conv, below = conv_terms(a1_ref[...], 1, UPPER_DILATION, unscaled)
    taps = kern_ref[1] * gain_ref[1][None, :]
    scaled = taps[0] * above + taps[1] * conv + taps[2] * below
    mean = jnp.mean(scaled * unscaled, axis=-1, keepdims=True)
    inverse = inv_ref[:, :, :1]
    rows = up_ref[0]
    upstream = jnp.stack([rows[s : s + 1] for s in range(SEQS)])
    incoming = jnp.where(inverse > 0.0, upstream, 0.0) + inverse * (scaled - unscaled * mean)
    act_grad = incoming.astype(jnp.bfloat16) * d0_ref[...]
    sum_ref[...] += lax.dot_general(
        m0_ref[...].reshape(tokens, width),
        act_grad.reshape(tokens, width),
        (((0,), (0,)), ((), ())),
        preferred_element_type=jnp.float32,
    )
    conv_terms(act_grad, 0, LOWER_DILATION, n0_ref[...].astype(jnp.float32))

    @pl.when(step == steps - 1)
    def _():
        spare = mine0.shape[1] - width
        for h in range(2):
            mine0[h, :width] = sum_ref[:, h * cols : (h + 1) * cols].astype(jnp.bfloat16)
            if spare:
                mine0[h, width:] = jnp.zeros((spare, cols), jnp.bfloat16)
        lower.pair_copy().start()
        rows = []
        for b in range(2):
            plain = jnp.sum(sums_ref[b], axis=1)
            rows.append(plain * gain_ref[b][None, :])
            rows.append(jnp.sum(plain * kern_ref[b], axis=0, keepdims=True))
        small = jnp.concatenate([rows[0], rows[2], rows[1], rows[3]], axis=0)
        for h in range(2):
            small_mine[h] = small[:, h * cols : (h + 1) * cols]
        small_copy = lower.copy(
            small_mine.at[other], small_pair, small_pair_sems.at[0], small_pair_sems.at[1], twin
        )
        small_copy.start()
        lower.pair_sum()
        lower.start_scatter()
        small_copy.wait_recv()
        small_slots[me] = small_mine[core] + small_pair[...]

        def small_send_to(k):
            return lower.copy(
                small_slots.at[me], small_slots.at[me], small_send.at[k], small_recv.at[me],
                lower.device_of(lower.peer(k)),
            )

        @pl.loop(1, chips)
        def _(k):
            small_send_to(k).start()

        upper.finish_gather()
        lower.finish_scatter()
        lower.start_gather()

        @pl.loop(1, chips)
        def _(k):
            chip = lower.peer(k)
            lower.copy(
                small_slots.at[chip], small_slots.at[chip], small_send.at[k],
                small_recv.at[chip], lower.device_of(chip),
            ).wait_recv()

        small_full[core] = lax.fori_loop(
            0, chips, lambda c, acc: acc + small_slots[c], jnp.zeros((8, cols), jnp.float32)
        )

        def small_forward(side):
            return lower.copy(
                small_full.at[side], small_full.at[side], small_last.at[0], small_last.at[1], twin
            )

        small_forward(core).start()
        upper.finish_last()
        for h in range(2):
            side = slice(h * cols, (h + 1) * cols)
            point_out[1, :, side] = full1[h, :width]
            head_out[h] = full1[h, width : width + head_rows]
        lower.finish_gather()
        small_forward(other).wait_recv()
        for h in range(2):
            side = slice(h * cols, (h + 1) * cols)
            depth_out[0, :, side] = small_full[h, 0:3]
            depth_out[1, :, side] = small_full[h, 3:6]
            gain_out[:, side] = small_full[h, 6:8]
        lower.finish_last()
        for h in range(2):
            point_out[0, :, h * cols : (h + 1) * cols] = full0[h, :width]
        upper.finish_sends()
        lower.finish_sends()
        small_copy.wait_send()
        small_forward(core).wait_send()

        @pl.loop(1, chips)
        def _(k):
            small_send_to(k).wait_send()


def run_lower(n_neg, n_rep, saved, pooled_grad, kernels, gains, weights, point1, head):
    total, length, width = saved[0].shape
    steps = total // SEQS
    assert steps >= 5
    chips = n_neg * n_rep // 2
    cols = width // 2
    grain = 16 * chips
    rows1 = -(-(width + head.shape[1]) // grain) * grain
    rows0 = -(-width // grain) * grain
    block = pl.BlockSpec((SEQS, length, width), lambda i: (i, 0, 0))
    whole = lambda shape: pl.BlockSpec(shape, lambda i: (0,) * len(shape))
    dma = pltpu.SemaphoreType.DMA

    def buffers(rows):
        return [
            pltpu.VMEM((2, rows, cols), jnp.bfloat16),
            pltpu.VMEM((rows, cols), jnp.bfloat16),
            pltpu.VMEM((chips, rows // chips, cols), jnp.bfloat16),
            pltpu.VMEM((2, rows, cols), jnp.bfloat16),
        ]

    outs = [
        jax.ShapeDtypeStruct(weights.shape, jnp.bfloat16),
        jax.ShapeDtypeStruct(head.shape, jnp.bfloat16),
        jax.ShapeDtypeStruct(kernels.shape, jnp.float32),
        jax.ShapeDtypeStruct(gains.shape, jnp.float32),
    ]
    return pl.pallas_call(
        functools.partial(lower_kernel, n_neg, n_rep, steps),
        grid=(steps,),
        in_specs=[block] * 5
        + [
            pl.BlockSpec((SEQS, length, 128), lambda i: (i, 0, 0)),
            pl.BlockSpec((1, 8, width), lambda i: (i, 0, 0)),
            whole(kernels.shape),
            whole(gains.shape),
            whole(weights.shape),
            whole(point1.shape),
            whole(head.shape),
        ],
        out_specs=[whole(out.shape) for out in outs],
        out_shape=outs,
        scratch_shapes=[
            pltpu.VMEM((width, width), jnp.float32),
            pltpu.VMEM((2, 3, 8, width), jnp.float32),
            *buffers(rows1),
            *buffers(rows0),
            pltpu.VMEM((2, 8, cols), jnp.float32),
            pltpu.VMEM((8, cols), jnp.float32),
            pltpu.VMEM((chips, 8, cols), jnp.float32),
            pltpu.VMEM((2, 8, cols), jnp.float32),
            *([dma((2,))] + [dma((chips,))] * 6),
            *([dma((2,))] + [dma((chips,))] * 6),
            dma((2,)),
            dma((chips,)),
            dma((chips,)),
            dma((2,)),
        ],
        compiler_params=pltpu.CompilerParams(
            collective_id=1, has_side_effects=True, vmem_limit_bytes=VMEM_LIMIT
        ),
    )(*saved, pooled_grad, kernels, gains, weights, point1, head)


def widen_kernel(point_ref, head_ref, loss_ref, point_out, head_out, loss_out):
    point_out[...] = point_ref[...].astype(jnp.float32)
    head_out[...] = head_ref[0].astype(jnp.float32)
    loss_out[...] = loss_ref[...]


def run_widen(point, head, loss):
    _, width, embed = head.shape
    part = point.shape[1] // 2
    rows = width // 2
    return pl.pallas_call(
        widen_kernel,
        grid=(4,),
        in_specs=[
            pl.BlockSpec((1, part, point.shape[2]), lambda i: (i // 2, i % 2, 0)),
            pl.BlockSpec((1, rows, embed), lambda i: (i // 2, i % 2, 0)),
            pl.BlockSpec(loss.shape, lambda i: (0, 0)),
        ],
        out_specs=[
            pl.BlockSpec((1, part, point.shape[2]), lambda i: (i // 2, i % 2, 0)),
            pl.BlockSpec((rows, embed), lambda i: (i, 0)),
            pl.BlockSpec(loss.shape, lambda i: (0, 0)),
        ],
        out_shape=[
            jax.ShapeDtypeStruct(point.shape, jnp.float32),
            jax.ShapeDtypeStruct((2 * width, embed), jnp.float32),
            jax.ShapeDtypeStruct(loss.shape, jnp.float32),
        ],
    )(point, head, loss)


def local(
    n_neg,
    n_rep,
    goal_states,
    premise_states,
    goal_ids,
    premise_ids,
    positives,
    kernels,
    gains,
    weights,
    head_weight,
):
    goals, premises = goal_states[0], premise_states[0]
    goal_count, length, width = goals.shape
    total = goal_count + premises.shape[0]
    ids = jnp.concatenate([goal_ids[0], premise_ids[0]], axis=0)
    lens = jnp.sum((ids != 0).astype(jnp.int32), axis=1)
    n0, m0, d0, n1, m1, d1, inverse, pooled = run_forward(
        lens, goals, premises, kernels, gains, weights
    )
    loss, pooled_grad, head = run_contrast(n_neg, goal_count, pooled, head_weight, positives)
    act1, upstream, point1 = run_upper(lens, m1, d1, pooled_grad)
    point, head, depth, gain = run_lower(
        n_neg, n_rep, (n0, m0, d0, n1, act1, inverse), upstream, kernels, gains, weights,
        point1, head,
    )
    point, head, loss = run_widen(point, head, loss)
    return loss, depth, gain, point, head


def solution(mesh):
    placed = (
        P("rep", "neg", None, None),
        P("rep", "neg", None, None),
        P("rep", "neg", None),
        P("rep", "neg", None),
        P("rep", None),
        P(),
        P(),
        P(),
        P(),
    )
    return jax.shard_map(
        functools.partial(local, mesh.shape["neg"], mesh.shape["rep"]),
        mesh=mesh,
        in_specs=placed,
        out_specs=(P("rep", "neg"), P(), P(), P(), P()),
        check_vma=False,
    )
```
